512 devices in a mesh: req: 32 (over y, z_lo), tp: 16 (over x, z_hi, core).
Axes of the slice: x: 4, y: 4, z: 16 (z_hi: 2, z_lo: 8; z = z_hi * 8 + z_lo), core: 2. Of those that a mesh axis runs over, the one named last changes fastest.
Arguments:
- state: float32 [384, 32, 128, 128], P('req', 'tp'), may hold values from -4 to 4
- conv_state: float32 [384, 16, 3, 512], P('req', 'tp'), may hold values from -6 to 6
- mixed: bfloat16 [384, 4, 16, 512], P('req', None, 'tp'), may hold values from -6 to 6
- gates: float32 [384, 4, 2, 32], P('req', None, None, 'tp'), may hold values from -6 to 6
- output_gate: bfloat16 [384, 4, 4096], P('req', None, 'tp'), may hold values from -6 to 6
- conv_weight: float32 [16, 4, 512], P('tp'), may hold values from -3 to 3
- decay_log: float32 [32], P('tp'), may hold values from -1.5 to 1.5
- time_bias: float32 [32], P('tp'), may hold values from -2 to 1
- norm_gain: float32 [128], replicated, may hold values from 0.25 to 1.75
- out_weight: bfloat16 [4096, 2048], P('tp'), may hold values from -0.09375 to 0.09375
- partner: int32 [32, 3], replicated, may hold values from 0 to 31, as said below
- moved_slots: int32 [32, 3], P('req'), may hold values from 0 to 11, as said below
Outputs:
- hidden_out: bfloat16 [384, 4, 2048], P('req')
- new_state: float32 [384, 32, 128, 128], P('req', 'tp')
- new_conv_state: float32 [384, 16, 3, 512], P('req', 'tp')
The draws below stay inside these ranges and needn't reach their ends.
Inputs may be any that keep to these rules, and one draw needn't show every extreme that they name: partner[g, j] = g XOR m_j, where each m_j lies in 1 to 31 and is common to all groups. `moved_slots`: each row holds 3 different slots.
All inputs are finite; a program needn't handle non-finite values.
Results may differ from the reference program's by a relative error of at most 0.0075.
Values may be sent and summed in bfloat16 or wider, within the bound.
A program may use at most 128 MiB of HBM per device.

```python
import jax
import jax.numpy as jnp
from jax import lax

D = 2048
KH = 16
VH = 32
DK = 128
DV = 128
TAPS = 4
STEPS = 4
REQ_DEV = 12
MOVE = 3
GROUPS = 32
REQUESTS = 384


def draw_partner(key, part):
    key = jax.random.fold_in(key, 1)
    groups_idx = jnp.arange(GROUPS, dtype=jnp.int32)
    offsets = jax.random.randint(key, (MOVE,), 1, GROUPS, dtype=jnp.int32)
    return jnp.bitwise_xor(groups_idx[:, None], offsets[None, :]).astype(jnp.int32)


def draw_moved_slots(key, part):
    key = jax.random.fold_in(key, 2)
    keys = jax.random.split(key, GROUPS)

    def one_row(row_key):
        return jax.random.permutation(row_key, REQ_DEV)[:MOVE]
    return jax.vmap(one_row)(keys).astype(jnp.int32)


def level_of(key, extent, shards, smallest, largest):
    loudness = 1.0
    for axis_at, blocks in shards:
        heights = jax.random.uniform(jax.random.fold_in(jax.random.fold_in(key, 6), axis_at), (blocks,), jnp.float32, smallest / len(shards), largest / len(shards))
        loudness = loudness * jnp.repeat(jnp.exp(heights), extent[axis_at] // blocks).reshape((-1,) + (1,) * (len(extent) - 1 - axis_at))
    return loudness


def scatter_about(rng, extent, scale, bound, pieces=(), held_as=jnp.bfloat16):
    values = scale * jax.random.normal(rng, extent, jnp.float32)
    if pieces:
        values = values * level_of(rng, extent, pieces, -0.22, 0.18)
    return jnp.clip(values, -bound, bound).astype(held_as)


def setup_inputs(seed: int = 0) -> dict:
    key_list = jax.random.split(jax.random.key(seed), 13)
    state = scatter_about(key_list[0], (REQUESTS, VH, DK, DV), 0.5, 4.0, ((0, 32), (1, 16)), jnp.float32)
    conv_state = scatter_about(key_list[1], (REQUESTS, KH, TAPS - 1, 4 * DK), 1.0, 6.0, ((0, 32), (1, 16)), jnp.float32)
    mixed = scatter_about(key_list[2], (REQUESTS, STEPS, KH, 4 * DK), 1.0, 6.0, ((0, 32), (2, 16)))
    gates = scatter_about(key_list[3], (REQUESTS, STEPS, 2, VH), 1.5, 6.0, ((0, 32), (3, 16)), jnp.float32)
    output_gate = scatter_about(key_list[4], (REQUESTS, STEPS, VH * DV), 1.0, 6.0, ((0, 32), (2, 16)))
    conv_weight = scatter_about(key_list[5], (KH, TAPS, 4 * DK), 0.5, 3.0, ((0, 16),), jnp.float32)
    decay_log = jnp.clip(jax.random.uniform(key_list[6], (VH,), jnp.float32, -1.5, 1.5) * level_of(key_list[6], (VH,), ((0, 16),), -0.4, 0.0), -1.5, 1.5)
    time_bias = jnp.clip(-2.0 + 3.0 * jax.random.uniform(key_list[7], (VH,), jnp.float32) ** level_of(key_list[7], (VH,), ((0, 16),), -0.2, 0.2), -2.0, 1.0)
    norm_gain = jnp.clip(1.0 + 0.15 * jax.random.normal(key_list[8], (DV,), jnp.float32), 0.25, 1.75)
    out_weight = scatter_about(key_list[9], (VH * DV, D), (VH * DV) ** -0.5, 0.09375, ((0, 16),))
    partner = draw_partner(jax.random.fold_in(key_list[12], 71), 0)
    moved_slots = draw_moved_slots(jax.random.fold_in(key_list[12], 71), 0)
    return {"state": state, "conv_state": conv_state, "mixed": mixed, "gates": gates, "output_gate": output_gate, "conv_weight": conv_weight, "decay_log": decay_log, "time_bias": time_bias, "norm_gain": norm_gain, "out_weight": out_weight, "partner": partner, "moved_slots": moved_slots}


def advance(state, conv_state, mixed, gates, output_gate, conv_weight, decay_log, time_bias, norm_gain):
    rows = mixed.shape[0]
    width = mixed.shape[3] // 4
    value_heads = state.shape[1]
    scale_a = jnp.exp(decay_log)
    gathered = []
    for step in range(mixed.shape[1]):
        latest = mixed[:, step].astype(jnp.float32)
        window = jnp.concatenate([conv_state, latest[:, :, None, :]], axis=2)
        conv = jax.nn.silu(lax.optimization_barrier(jnp.sum(window * conv_weight[None], axis=2)))
        conv_state = window[:, :, 1:]
        query = conv[..., :width]
        keyvec = conv[..., width:2 * width]
        values = conv[..., 2 * width:].reshape(rows, value_heads, -1)
        query = query * lax.rsqrt(lax.optimization_barrier(jnp.sum(query * query, -1, keepdims=True)) + 1e-06) / jnp.sqrt(jnp.float32(width))
        keyvec = keyvec * lax.rsqrt(lax.optimization_barrier(jnp.sum(keyvec * keyvec, -1, keepdims=True)) + 1e-06)
        query = jnp.repeat(query, 2, axis=1)
        keyvec = jnp.repeat(keyvec, 2, axis=1)
        decay = jnp.exp(-scale_a * jax.nn.softplus(gates[:, step, 0] + time_bias))
        beta = jax.nn.sigmoid(gates[:, step, 1])
        state = state * decay[..., None, None]
        readout = jnp.einsum('nhk,nhkv->nhv', keyvec, state, precision=lax.Precision.HIGHEST)
        delta = (values - readout) * beta[..., None]
        state = state + keyvec[..., :, None] * delta[..., None, :]
        result = jnp.einsum('nhk,nhkv->nhv', query, state, precision=lax.Precision.HIGHEST)
        zvalue = output_gate[:, step].astype(jnp.float32).reshape(rows, value_heads, -1)
        normed = result * lax.rsqrt(lax.optimization_barrier(jnp.mean(result * result, -1, keepdims=True)) + 1e-06)
        gated = (normed * norm_gain * jax.nn.silu(zvalue)).astype(jnp.bfloat16)
        gathered.append(gated.reshape(rows, -1))
    return (jnp.stack(gathered, axis=1), state, conv_state)

def migrate(whole, partner, moved_slots):
    grouped = whole.reshape((GROUPS, REQ_DEV) + whole.shape[1:])
    column = jnp.arange(MOVE, dtype=jnp.int32)[None, :]
    source = grouped[partner, moved_slots[partner, column]]
    rows_idx = jnp.arange(GROUPS, dtype=jnp.int32)[:, None]
    grouped = grouped.at[rows_idx, moved_slots].set(source)
    return grouped.reshape(whole.shape)

def reference(state, conv_state, mixed, gates, output_gate, conv_weight, decay_log, time_bias, norm_gain, out_weight, partner, moved_slots):
    state = migrate(state, partner, moved_slots)
    conv_state = migrate(conv_state, partner, moved_slots)
    gated, state, conv_state = advance(state, conv_state, mixed, gates, output_gate, conv_weight, decay_log, time_bias, norm_gain)
    flat = gated.reshape(-1, gated.shape[-1])
    hidden_out = jnp.dot(flat, out_weight, preferred_element_type=jnp.float32).astype(jnp.bfloat16)
    hidden_out = hidden_out.reshape(gated.shape[0], gated.shape[1], -1)
    return (hidden_out, state, conv_state)
```

```python
import functools

import jax
import jax.numpy as jnp
from jax import lax
from jax.experimental import pallas as pl
from jax.experimental.pallas import tpu as pltpu
from jax.sharding import PartitionSpec as P

MESH = pl.DeviceIdType.MESH
F32 = jnp.float32
BF16 = jnp.bfloat16
GROUPS, MOVE, PIECES, TILE, LANES = 32, 3, 16, 16, 128
CONV_PIECE = (2, 7, 12)
VMEM = pltpu.VMEM
HEAD = 128


def piece_holder(piece, core):
    return 2 * piece + lax.rem(core + piece // 4, 2)


def migrate_kernel(
    state, conv, partner, slots, out,
    rows_out, conv_rows, conv_out, held, conv_held, turned, conv_turned, landed, conv_landed,
    send1, recv1, csend1, crecv1, send2, recv2, csend2, crecv2,
):
    me = lax.axis_index("req")
    core = lax.rem(lax.axis_index("tp"), 2)
    mine = me // 2
    holder = piece_holder(mine, core) == me

    barrier = pltpu.get_barrier_semaphore()

    def greet(k, carry):
        peer = lax.rem(me + k, GROUPS)
        pl.semaphore_signal(barrier, inc=1, device_id={"req": peer}, device_id_type=MESH)
        return carry

    lax.fori_loop(1, GROUPS, greet, 0)

    conv_rows[...] = jnp.zeros_like(conv_rows)
    for j in range(MOVE):
        slot = slots[0, j]
        for tap in range(3):
            for part in range(4):
                conv_rows[j, pl.ds(tap * 4 + part, 1), :] = conv[
                    slot, tap, :, part * LANES : (part + 1) * LANES
                ]
        conv_out[j] = conv_rows[j].astype(BF16)

    def pack(piece, carry):
        for j in range(MOVE):
            start = pl.multiple_of(lax.rem(piece, 8) * TILE, TILE)
            rows_out[piece, j] = state[slots[0, j], piece // 8, pl.ds(start, TILE), :].astype(BF16)
        return carry

    lax.fori_loop(0, PIECES, pack, 0)
    pl.semaphore_wait(barrier, GROUPS - 1)

    def first(piece, peer):
        return pltpu.make_async_remote_copy(
            src_ref=rows_out.at[piece], dst_ref=held.at[me], send_sem=send1.at[piece],
            recv_sem=recv1.at[me], device_id={"req": peer}, device_id_type=MESH,
        )

    def conv_first(j, peer):
        return pltpu.make_async_remote_copy(
            src_ref=conv_out.at[j], dst_ref=conv_held.at[me], send_sem=csend1.at[j],
            recv_sem=crecv1.at[me], device_id={"req": peer}, device_id_type=MESH,
        )

    def send_piece(k, carry):
        piece = lax.rem(mine + k, PIECES)
        peer = piece_holder(piece, core)

        @pl.when(peer != me)
        def _():
            first(piece, peer).start()

        @pl.when(peer == me)
        def _():
            held[me] = rows_out[piece]

        return carry

    lax.fori_loop(0, PIECES, send_piece, 0)
    for j in range(MOVE):
        peer = piece_holder(CONV_PIECE[j], core)

        @pl.when(peer != me)
        def _():
            conv_first(j, peer).start()

        @pl.when(peer == me)
        def _():
            conv_held[me] = conv_out[j]

    def second(dest):
        return pltpu.make_async_remote_copy(
            src_ref=turned.at[dest], dst_ref=landed.at[mine], send_sem=send2.at[dest],
            recv_sem=recv2.at[mine], device_id={"req": dest}, device_id_type=MESH,
        )

    def conv_second(j, dest):
        return pltpu.make_async_remote_copy(
            src_ref=conv_turned.at[dest], dst_ref=conv_landed.at[j], send_sem=csend2.at[dest],
            recv_sem=crecv2.at[j], device_id={"req": dest}, device_id_type=MESH,
        )

    def arrived(group):
        return pltpu.make_async_remote_copy(
            src_ref=rows_out.at[0], dst_ref=held.at[group], send_sem=send1.at[0],
            recv_sem=recv1.at[group], device_id={"req": group}, device_id_type=MESH,
        )

    def conv_arrived(group):
        return pltpu.make_async_remote_copy(
            src_ref=conv_out.at[0], dst_ref=conv_held.at[group], send_sem=csend1.at[0],
            recv_sem=crecv1.at[group], device_id={"req": group}, device_id_type=MESH,
        )

    @pl.when(holder)
    def _():
        def wait_first(k, carry):
            arrived(lax.rem(me + k, GROUPS)).wait_recv()
            return carry

        lax.fori_loop(1, GROUPS, wait_first, 0)

        def turn(k, carry):
            dest = lax.rem(me + k, GROUPS)
            for j in range(MOVE):
                turned[dest, j] = held[partner[j, dest], j]

            @pl.when(k > 0)
            def _():
                second(dest).start()

            return carry

        lax.fori_loop(0, GROUPS, turn, 0)
        landed[mine] = turned[me]

        for j in range(MOVE):

            @pl.when(mine == CONV_PIECE[j])
            def _():
                def wait_conv(k, carry):
                    conv_arrived(lax.rem(me + k, GROUPS)).wait_recv()
                    return carry

                lax.fori_loop(1, GROUPS, wait_conv, 0)

                def turn_conv(k, carry):
                    dest = lax.rem(me + k, GROUPS)
                    conv_turned[dest] = conv_held[partner[j, dest]]

                    @pl.when(k > 0)
                    def _():
                        conv_second(j, dest).start()

                    return carry

                lax.fori_loop(0, GROUPS, turn_conv, 0)
                conv_landed[j] = conv_turned[me]

    def wait_second(piece, carry):
        source = piece_holder(piece, core)

        @pl.when(source != me)
        def _():
            pltpu.make_async_remote_copy(
                src_ref=turned.at[0], dst_ref=landed.at[piece], send_sem=send2.at[0],
                recv_sem=recv2.at[piece], device_id={"req": source}, device_id_type=MESH,
            ).wait_recv()

        start = pl.multiple_of(piece * TILE, TILE)
        for j in range(MOVE):
            out[j, pl.ds(start, TILE), :] = landed[piece, j]
        return carry

    lax.fori_loop(0, PIECES, wait_second, 0)
    for j in range(MOVE):
        source = piece_holder(CONV_PIECE[j], core)

        @pl.when(source != me)
        def _():
            conv_second(j, source).wait_recv()

        out[j, PIECES * TILE :, :] = conv_landed[j]

    def done_first(piece, carry):
        peer = piece_holder(piece, core)

        @pl.when(peer != me)
        def _():
            first(piece, peer).wait_send()

        return carry

    lax.fori_loop(0, PIECES, done_first, 0)
    for j in range(MOVE):
        peer = piece_holder(CONV_PIECE[j], core)

        @pl.when(peer != me)
        def _():
            conv_first(j, peer).wait_send()

    @pl.when(holder)
    def _():
        def done_second(k, carry):
            second(lax.rem(me + k, GROUPS)).wait_send()
            return carry

        lax.fori_loop(1, GROUPS, done_second, 0)
        for j in range(MOVE):

            @pl.when(mine == CONV_PIECE[j])
            def _():
                def done_conv(k, carry):
                    conv_second(j, lax.rem(me + k, GROUPS)).wait_send()
                    return carry

                lax.fori_loop(1, GROUPS, done_conv, 0)


def migrate(state, conv, partner, slots):
    tile = (TILE, LANES)
    dma = pltpu.SemaphoreType.DMA
    return pl.pallas_call(
        migrate_kernel,
        out_shape=jax.ShapeDtypeStruct((MOVE, (PIECES + 1) * TILE, LANES), BF16),
        in_specs=[
            pl.BlockSpec(memory_space=VMEM),
            pl.BlockSpec(memory_space=VMEM),
            pl.BlockSpec(memory_space=pltpu.SMEM),
            pl.BlockSpec(memory_space=pltpu.SMEM),
        ],
        out_specs=pl.BlockSpec(memory_space=VMEM),
        scratch_shapes=[
            VMEM((PIECES, MOVE) + tile, BF16),
            VMEM((MOVE,) + tile, F32),
            VMEM((MOVE,) + tile, BF16),
            VMEM((GROUPS, MOVE) + tile, BF16),
            VMEM((GROUPS,) + tile, BF16),
            VMEM((GROUPS, MOVE) + tile, BF16),
            VMEM((GROUPS,) + tile, BF16),
            VMEM((PIECES, MOVE) + tile, BF16),
            VMEM((MOVE,) + tile, BF16),
            dma((PIECES,)), dma((GROUPS,)), dma((MOVE,)), dma((GROUPS,)),
            dma((GROUPS,)), dma((PIECES,)), dma((GROUPS,)), dma((MOVE,)),
        ],
        compiler_params=pltpu.CompilerParams(
            collective_id=0, has_side_effects=True, vmem_limit_bytes=32 << 20
        ),
        name="migrate",
    )(state, conv, partner, slots)


def halves(scalar_a, scalar_b, shape):
    lane = lax.broadcasted_iota(jnp.int32, shape, len(shape) - 1)
    return jnp.where(lane < HEAD, scalar_a, scalar_b)


def split16(value):
    high = value.astype(BF16)
    return high.astype(F32), value - high.astype(F32)


def advance_kernel(
    slots, decay_log, time_bias, state, came, conv, mixed, gates, zgate, weight, gain,
    new_state, new_conv, gated,
    taps, fresh, gate_rows, left, right, solved, flat, sems,
):
    rows = mixed.shape[0]
    copies = [
        pltpu.make_async_copy(state.at[pl.ds(2 * i, 2)], new_state.at[pl.ds(2 * i, 2)], sems.at[i])
        for i in range(rows // 2)
    ]
    for copy in copies:
        copy.start()

    for tap in range(3):
        taps[tap] = conv[:, tap]
    for j in range(MOVE):
        slot = slots[0, j]
        tile = came[j, PIECES * TILE :, :].astype(F32)
        for tap in range(3):
            for part in range(4):
                taps[tap, slot, :, part * LANES : (part + 1) * LANES] = tile[
                    tap * 4 + part : tap * 4 + part + 1, :
                ]
    fresh[...] = mixed[...].astype(F32)
    for tap in range(3):
        new_conv[:, tap, 0, :] = fresh[:, tap + 1, :]
    window = [taps[i, :, 0, :] for i in range(3)] + [fresh[:, t, :] for t in range(4)]

    gate_rows[...] = jnp.zeros_like(gate_rows)
    for t in range(4):
        for kind in range(2):
            at = t * 4 + kind * 2
            gate_rows[at : at + 2, 0:rows] = gates[t, kind]
    columns = gate_rows[...].T

    def column(at):
        return jnp.broadcast_to(columns[0:rows, at : at + 1], (rows, HEAD))

    def both(at):
        return jnp.concatenate([column(at), column(at + 1)], axis=1)

    rate = jnp.exp(halves(decay_log[0], decay_log[1], (1, 2 * HEAD)))
    bias = halves(time_bias[0], time_bias[1], (1, 2 * HEAD))
    keys, queries, values, decays, betas = [], [], [], [], []
    for t in range(4):
        total = window[t] * weight[0, 0:1, :]
        for tap in range(1, 4):
            total = total + window[t + tap] * weight[0, tap : tap + 1, :]
        c = total * jax.nn.sigmoid(total)
        q, k = c[:, :HEAD], c[:, HEAD : 2 * HEAD]
        queries.append(
            q * lax.rsqrt(jnp.sum(q * q, -1, keepdims=True) + 1e-06) / jnp.sqrt(jnp.float32(HEAD))
        )
        keys.append(k * lax.rsqrt(jnp.sum(k * k, -1, keepdims=True) + 1e-06))
        values.append(c[:, 2 * HEAD :])
        a = both(t * 4) + bias
        soft = jnp.maximum(a, 0.0) + jnp.log1p(jnp.exp(-jnp.abs(a)))
        decays.append(jnp.exp(-rate * soft))
        betas.append(jax.nn.sigmoid(both(t * 4 + 2)))

    left[...] = jnp.zeros_like(left)
    right[...] = jnp.zeros_like(right)
    key_parts = [split16(k) for k in keys]
    query_parts = [split16(q) for q in queries]
    for t in range(4):
        left[t, 0:rows, :] = key_parts[t][0]
        left[4 + t, 0:rows, :] = query_parts[t][0]
        left[8 + t, 0:rows, :] = key_parts[t][1]
        left[12 + t, 0:rows, :] = query_parts[t][1]

    for copy in copies:
        copy.wait()
    for j in range(MOVE):
        for h in range(2):
            new_state[slots[0, j], h] = came[j, h * HEAD : (h + 1) * HEAD, :].astype(F32)

    for r in range(rows):
        lhs = left[:, r, :].astype(BF16)
        for h in range(2):
            block = new_state[r, h]
            high = block.astype(BF16)
            low = (block - high.astype(F32)).astype(BF16)
            product = jnp.dot(lhs, high, preferred_element_type=F32) + jnp.dot(
                lhs, low, preferred_element_type=F32
            )
            solved[r, :, h * HEAD : (h + 1) * HEAD] = product[0:8] + product[8:16]

    writes = []
    carried = [decays[0]]
    for t in range(1, 4):
        carried.append(carried[-1] * decays[t])
    for t in range(4):
        read = solved[:, t, :] * carried[t]
        out = solved[:, 4 + t, :] * carried[t]
        writes = [w * decays[t] for w in writes]
        for s in range(t):
            read = read + writes[s] * jnp.sum(keys[t] * keys[s], -1, keepdims=True)
            out = out + writes[s] * jnp.sum(queries[t] * keys[s], -1, keepdims=True)
        writes.append((values[t] - read) * betas[t])
        out = out + writes[t] * jnp.sum(queries[t] * keys[t], -1, keepdims=True)
        square = out * out
        norm = jnp.concatenate(
            [
                jnp.broadcast_to(
                    lax.rsqrt(
                        jnp.mean(square[:, h * HEAD : (h + 1) * HEAD], -1, keepdims=True) + 1e-06
                    ),
                    (rows, HEAD),
                )
                for h in range(2)
            ],
            axis=1,
        )
        z = zgate[:, t, :].astype(F32)
        spread = jnp.concatenate([gain[...], gain[...]], axis=1)
        result = out * norm * spread * (z * jax.nn.sigmoid(z))
        for h in range(2):
            flat[h, pl.ds(t, rows, stride=4), :] = result[:, h * HEAD : (h + 1) * HEAD]
    for h in range(2):
        gated[:, h * HEAD : (h + 1) * HEAD] = flat[h].astype(BF16)

    left[12:16] = jnp.zeros_like(left[12:16])
    for t in range(4):
        left[4 + t, 0:rows, :] = key_parts[t][0]
        high, low = split16(writes[t])
        right[t, 0:rows, :] = high
        right[4 + t, 0:rows, :] = low
        right[8 + t, 0:rows, :] = high
    right[12, 0:rows, :] = carried[3]

    for r in range(rows):
        lhs = left[:, r, :].astype(BF16)
        rhs = right[:, r, :]
        update = lax.dot_general(
            lhs, rhs.astype(BF16), (((0,), (0,)), ((), ())), preferred_element_type=F32
        )
        for h in range(2):
            cut = slice(h * HEAD, (h + 1) * HEAD)
            new_state[r, h] = new_state[r, h] * rhs[12:13, cut] + update[:, cut]


def advance(slots, decay_log, time_bias, state, came, conv, mixed, gates, zgate, weight, gain):
    rows = state.shape[0]
    vmem = pl.BlockSpec(memory_space=VMEM)
    smem = pl.BlockSpec(memory_space=pltpu.SMEM)
    return pl.pallas_call(
        advance_kernel,
        out_shape=(
            jax.ShapeDtypeStruct(state.shape, F32),
            jax.ShapeDtypeStruct(conv.shape, F32),
            jax.ShapeDtypeStruct((rows * 4, 2 * HEAD), BF16),
        ),
        in_specs=[smem, smem, smem, pl.BlockSpec(memory_space=pl.ANY)] + [vmem] * 7,
        out_specs=(vmem, vmem, vmem),
        scratch_shapes=[
            VMEM((3, rows, 1, 4 * HEAD), F32),
            VMEM(mixed.shape, F32),
            VMEM((LANES, LANES), F32),
            VMEM((16, 16, HEAD), F32),
            VMEM((16, 16, 2 * HEAD), F32),
            VMEM((rows, 8, 2 * HEAD), F32),
            VMEM((2, rows * 4, HEAD), F32),
            pltpu.SemaphoreType.DMA((rows // 2,)),
        ],
        compiler_params=pltpu.CompilerParams(vmem_limit_bytes=32 << 20),
        name="advance",
    )(slots, decay_log, time_bias, state, came, conv, mixed, gates, zgate, weight, gain)


def reduce_kernel(
    gated, weight, out,
    give, own, got, pass_on, passed, half, half_got, blocks,
    give_send, give_recv, pass_send, pass_recv, half_send, half_recv,
    ring_send, ring_recv, mate_send, mate_recv,
):
    tp = lax.axis_index("tp")
    x, high, core = tp // 4, lax.rem(tp // 2, 2), lax.rem(tp, 2)
    mate = x * 4 + high * 2 + (1 - core)
    far = x * 4 + (1 - high) * 2 + core
    width = give.shape[2]

    def at_x(k):
        return lax.rem(x + k, 4)

    def ring(k):
        return at_x(k) * 4 + high * 2 + core

    barrier = pltpu.get_barrier_semaphore()
    for peer in (mate, far, ring(1), ring(2), ring(3)):
        pl.semaphore_signal(barrier, inc=1, device_id={"tp": peer}, device_id_type=MESH)

    def term(block):
        cut = pl.ds(pl.multiple_of(block * width, width), width)
        return jnp.dot(gated[...], weight[:, cut], preferred_element_type=F32)

    def to(peer, src, dst, send, recv):
        return pltpu.make_async_remote_copy(
            src_ref=src, dst_ref=dst, send_sem=send, recv_sem=recv,
            device_id={"tp": peer}, device_id_type=MESH,
        )

    order = (2, 1, 3, 0)
    gives = [to(mate, give.at[k], got.at[k], give_send.at[k], give_recv.at[k]) for k in range(4)]
    for k in order:
        give[k] = term(at_x(k) * 2 + 1 - core).astype(BF16)
        if k == order[0]:
            pl.semaphore_wait(barrier, 5)
        gives[k].start()
    for k in order:
        own[k] = term(at_x(k) * 2 + core)
    passes = [
        to(ring(k), pass_on.at[k - 1], passed.at[k - 1], pass_send.at[k - 1], pass_recv.at[k - 1])
        for k in range(1, 4)
    ]
    for k in order:
        gives[k].wait_recv()
        total = own[k] + got[k].astype(F32)
        if k:
            pass_on[k - 1] = total.astype(BF16)
            passes[k - 1].start()
    for k in range(1, 4):
        passes[k - 1].wait_recv()
        total = total + passed[k - 1].astype(F32)
    half[...] = total.astype(BF16)
    swap = to(far, half, half_got, half_send, half_recv)
    swap.start()
    swap.wait_recv()
    mine = x * 2 + core
    blocks[mine] = (half[...].astype(F32) + half_got[...].astype(F32)).astype(BF16)
    rings = [
        to(ring(k), blocks.at[mine], blocks.at[mine], ring_send.at[k - 1], ring_recv.at[k - 1])
        for k in range(1, 4)
    ]
    mates = [
        to(mate, blocks.at[at_x(k) * 2 + core], blocks.at[at_x(k) * 2 + core],
           mate_send.at[k], mate_recv.at[k])
        for k in range(4)
    ]
    for k in (2, 1, 3):
        rings[k - 1].start()
    mates[0].start()
    for k in range(1, 4):
        rings[k - 1].wait_recv()
        mates[4 - k].start()
    for k in range(4):
        mates[k].wait_recv()
    for block in range(8):
        out[:, block * width : (block + 1) * width] = blocks[block]
    for copy in gives + passes + [swap] + rings + mates:
        copy.wait_send()


def reduce_terms(gated, weight):
    rows, cols = gated.shape[0], weight.shape[1]
    block = (rows, cols // 8)
    vmem = pl.BlockSpec(memory_space=VMEM)
    dma = pltpu.SemaphoreType.DMA
    return pl.pallas_call(
        reduce_kernel,
        out_shape=jax.ShapeDtypeStruct((rows, cols), BF16),
        in_specs=[vmem, vmem],
        out_specs=vmem,
        scratch_shapes=[
            VMEM((4,) + block, BF16), VMEM((4,) + block, F32), VMEM((4,) + block, BF16),
            VMEM((3,) + block, BF16), VMEM((3,) + block, BF16),
            VMEM(block, BF16), VMEM(block, BF16), VMEM((8,) + block, BF16),
            dma((4,)), dma((4,)), dma((3,)), dma((3,)), dma, dma,
            dma((3,)), dma((3,)), dma((4,)), dma((4,)),
        ],
        compiler_params=pltpu.CompilerParams(
            collective_id=1, has_side_effects=True, vmem_limit_bytes=32 << 20
        ),
        name="reduce_terms",
    )(gated, weight)


def per_device(
    state,
    conv_state,
    mixed,
    gates,
    output_gate,
    conv_weight,
    decay_log,
    time_bias,
    norm_gain,
    out_weight,
    partner,
    moved_slots,
):
    conv = conv_state.transpose(0, 2, 1, 3)
    fresh = mixed.reshape(mixed.shape[0], mixed.shape[1], mixed.shape[3])
    gate_rows = gates.transpose(1, 2, 3, 0)
    came = migrate(state, conv, partner.T, moved_slots)
    new_state, new_conv, gated = advance(
        moved_slots, decay_log, time_bias, state, came, conv, fresh, gate_rows, output_gate,
        conv_weight, norm_gain.reshape(1, -1),
    )
    hidden = reduce_terms(gated, out_weight)
    hidden = hidden.reshape(mixed.shape[0], mixed.shape[1], -1)
    return (hidden, new_state, new_conv.transpose(0, 2, 1, 3))


def solution(mesh):
    placed = (
        P("req", "tp", None, None),
        P("req", "tp", None, None),
        P("req", None, "tp", None),
        P("req", None, None, "tp"),
        P("req", None, "tp"),
        P("tp", None, None),
        P("tp"),
        P("tp"),
        P(),
        P("tp", None),
        P(),
        P("req", None),
    )
    return jax.shard_map(
        per_device,
        mesh=mesh,
        in_specs=placed,
        out_specs=(P("req", None, None), P("req", "tp", None, None), P("req", "tp", None, None)),
        check_vma=False,
    )
```

```python
import jax
import jax.numpy as jnp
from jax import lax
from jax.experimental import pallas as pl
from jax.experimental.pallas import tpu as pltpu
from jax.sharding import PartitionSpec as P

MESH = pl.DeviceIdType.MESH
F32 = jnp.float32
BF16 = jnp.bfloat16
VMEM = pltpu.VMEM
GROUPS, MOVE, PIECES, TILE, LANES = 32, 3, 16, 16, 128
CONV_PIECE = (2, 7, 12)
HEAD, TAPS, STEPS = 128, 4, 4


def piece_holder(piece, core):
    return 2 * piece + lax.rem(core + piece // 4, 2)


def split16(value):
    high = value.astype(BF16)
    return high.astype(F32), value - high.astype(F32)


def halves(scalar_a, scalar_b, shape):
    lane = lax.broadcasted_iota(jnp.int32, shape, len(shape) - 1)
    return jnp.where(lane < HEAD, scalar_a, scalar_b)


def convolved(window, weight):
    queries, keys, values = [], [], []
    for t in range(STEPS):
        total = window[t] * weight[0, 0:1, :]
        for tap in range(1, TAPS):
            total = total + window[t + tap] * weight[0, tap : tap + 1, :]
        c = total * jax.nn.sigmoid(total)
        q, k = c[:, :HEAD], c[:, HEAD : 2 * HEAD]
        queries.append(
            q * lax.rsqrt(jnp.sum(q * q, -1, keepdims=True) + 1e-06) / jnp.sqrt(jnp.float32(HEAD))
        )
        keys.append(k * lax.rsqrt(jnp.sum(k * k, -1, keepdims=True) + 1e-06))
        values.append(c[:, 2 * HEAD :])
    return queries, keys, values


def read_side(left, queries, keys):
    rows = keys[0].shape[0]
    for t in range(STEPS):
        for at, part in enumerate(split16(keys[t]) + split16(queries[t])):
            left[t + (0, 8, 4, 12)[at], 0:rows, :] = part


def products(queries, keys):
    pairs = [(t, s) for t in range(STEPS) for s in range(t + 1)]
    written = {p: jnp.sum(keys[p[0]] * keys[p[1]], -1, keepdims=True) for p in pairs if p[0] != p[1]}
    read = {p: jnp.sum(queries[p[0]] * keys[p[1]], -1, keepdims=True) for p in pairs}
    return written, read


def solve(solved, flat, gram, values, decays, betas, zs, gain):
    rows = values[0].shape[0]
    key_key, query_key = gram
    writes = []
    carried = [decays[0]]
    for t in range(1, STEPS):
        carried.append(carried[-1] * decays[t])
    spread = jnp.concatenate([gain, gain], axis=1)
    for t in range(STEPS):
        read = solved[0:rows, t, :] * carried[t]
        out = solved[0:rows, 4 + t, :] * carried[t]
        writes = [w * decays[t] for w in writes]
        for s in range(t):
            read = read + writes[s] * key_key[t, s]
            out = out + writes[s] * query_key[t, s]
        writes.append((values[t] - read) * betas[t])
        out = out + writes[t] * query_key[t, t]
        square = out * out
        norm = jnp.concatenate(
            [
                jnp.broadcast_to(
                    lax.rsqrt(
                        jnp.mean(square[:, h * HEAD : (h + 1) * HEAD], -1, keepdims=True) + 1e-06
                    ),
                    (rows, HEAD),
                )
                for h in range(2)
            ],
            axis=1,
        )
        result = out * norm * spread * (zs[t] * jax.nn.sigmoid(zs[t]))
        for h in range(2):
            flat[h, pl.ds(t, rows, stride=STEPS), :] = result[:, h * HEAD : (h + 1) * HEAD]
    return writes, carried[-1]


def write_side(left, right, keys, writes, carried):
    rows = keys[0].shape[0]
    left[12:16] = jnp.zeros_like(left[12:16])
    for t in range(STEPS):
        high, low = split16(keys[t])
        left[t, 0:rows, :] = high
        left[4 + t, 0:rows, :] = high
        left[8 + t, 0:rows, :] = low
        high, low = split16(writes[t])
        right[t, 0:rows, :] = high
        right[4 + t, 0:rows, :] = low
        right[8 + t, 0:rows, :] = high
    right[12, 0:rows, :] = carried


def updated(left, right, row, blocks):
    lhs = left[:, row, :].astype(BF16)
    rhs = right[:, row, :]
    update = lax.dot_general(
        lhs, rhs.astype(BF16), (((0,), (0,)), ((), ())), preferred_element_type=F32
    )
    for h in range(2):
        cut = slice(h * HEAD, (h + 1) * HEAD)
        yield blocks[h] * rhs[12:13, cut] + update[:, cut]


class Reduction:
    def __init__(self, place, scratch, weight):
        self.x, self.high, self.core = place
        (
            self.give, self.own, self.got, self.pass_on, self.passed, self.half, self.half_got,
            self.blocks, gs, gr, ps, pr, hs, hr, rs, rr, ms, mr,
        ) = scratch
        self.weight = weight
        self.width = self.give.shape[2]
        mate, far = self.peers()[:2]
        self.gives = [self.to(mate, self.give.at[k], self.got.at[k], gs.at[k], gr.at[k]) for k in range(4)]
        self.passes = [
            self.to(self.ring(k), self.pass_on.at[k - 1], self.passed.at[k - 1], ps.at[k - 1], pr.at[k - 1])
            for k in range(1, 4)
        ]
        self.swap = self.to(far, self.half, self.half_got, hs, hr)
        self.mine = self.x * 2 + self.core
        own = self.blocks.at[self.mine]
        self.rings = [self.to(self.ring(k), own, own, rs.at[k - 1], rr.at[k - 1]) for k in range(1, 4)]
        self.mates = []
        for k in range(4):
            block = self.blocks.at[self.at_x(k) * 2 + self.core]
            self.mates.append(self.to(mate, block, block, ms.at[k], mr.at[k]))

    def peers(self):
        here = self.x * 4 + self.high * 2
        return (
            here + 1 - self.core, self.x * 4 + (1 - self.high) * 2 + self.core,
            self.ring(2), self.ring(1), self.ring(3),
        )

    def at_x(self, k):
        return lax.rem(self.x + k, 4)

    def ring(self, k):
        return self.at_x(k) * 4 + self.high * 2 + self.core

    def to(self, peer, src, dst, send, recv):
        return pltpu.make_async_remote_copy(
            src_ref=src, dst_ref=dst, send_sem=send, recv_sem=recv,
            device_id={"tp": peer}, device_id_type=MESH,
        )

    def term(self, gated, block):
        cut = pl.ds(pl.multiple_of(block * self.width, self.width), self.width)
        return jnp.dot(gated, self.weight[:, cut], preferred_element_type=F32)

    order = (2, 1, 3, 0)

    def begin(self, gated):
        for k in self.order:
            self.give[k] = self.term(gated, self.at_x(k) * 2 + 1 - self.core).astype(BF16)
            self.gives[k].start()
        for k in self.order:
            self.own[k] = self.term(gated, self.at_x(k) * 2 + self.core)

    def along_x(self):
        for k in self.order:
            self.gives[k].wait_recv()
            total = self.own[k] + self.got[k].astype(F32)
            if k:
                self.pass_on[k - 1] = total.astype(BF16)
                self.passes[k - 1].start()
            else:
                self.own[0] = total

    def along_z(self):
        total = self.own[0]
        for k in (1, 3, 2):
            self.passes[k - 1].wait_recv()
            total = total + self.passed[k - 1].astype(F32)
        self.half[...] = total.astype(BF16)
        self.swap.start()

    def back_x(self):
        self.swap.wait_recv()
        self.blocks[self.mine] = (self.half[...].astype(F32) + self.half_got[...].astype(F32)).astype(BF16)
        for k in (2, 1, 3):
            self.rings[k - 1].start()
        self.mates[0].start()

    def back_core(self):
        for k in (1, 3, 2):
            self.rings[k - 1].wait_recv()
            self.mates[4 - k].start()

    def end(self):
        for k in range(4):
            self.mates[k].wait_recv()

    def drain(self):
        for copy in self.gives + self.passes + [self.swap] + self.rings + self.mates:
            copy.wait_send()

    @staticmethod
    def scratch(rows, width):
        dma = pltpu.SemaphoreType.DMA
        block = (rows, width)
        return [
            VMEM((4,) + block, BF16), VMEM((4,) + block, F32), VMEM((4,) + block, BF16),
            VMEM((3,) + block, BF16), VMEM((3,) + block, BF16),
            VMEM(block, BF16), VMEM(block, BF16), VMEM((8,) + block, BF16),
            dma((4,)), dma((4,)), dma((3,)), dma((3,)), dma, dma,
            dma((3,)), dma((3,)), dma((4,)), dma((4,)),
        ]


class ShortReduction:
    def __init__(self, place, scratch, weight):
        self.x, self.high, self.core = place
        (
            self.give, self.own, self.got, self.half, self.half_got, self.blocks,
            gs, gr, hs, hr, bs, br,
        ) = scratch
        self.weight = weight
        self.width = self.give.shape[2]
        self.mine = self.x * 2 + self.core
        self.gives, self.backs, self.awaited = [], [], []
        for at, (dx, dc) in enumerate(self.order):
            peer = self.device(dx, dc)
            self.gives.append(self.to(peer, self.give.at[at], self.got.at[at], gs.at[at], gr.at[at]))
            own = self.blocks.at[self.mine]
            self.backs.append(self.to(peer, own, own, bs.at[at], br.at[at]))
            theirs = self.blocks.at[self.block(-dx, dc)]
            self.awaited.append(self.to(self.device(-dx, dc), own, theirs, bs.at[at], br.at[at]))
        far = self.x * 4 + (1 - self.high) * 2 + self.core
        self.swap = self.to(far, self.half, self.half_got, hs, hr)

    order = ((2, 0), (2, 1), (1, 0), (1, 1), (3, 0), (3, 1), (0, 1))

    def toward(self, dx, dc):
        return lax.rem(self.x + dx + 4, 4), 1 - self.core if dc else self.core

    def device(self, dx, dc):
        x, core = self.toward(dx, dc)
        return x * 4 + self.high * 2 + core

    def block(self, dx, dc):
        x, core = self.toward(dx, dc)
        return x * 2 + core

    def peers(self):
        far = self.x * 4 + (1 - self.high) * 2 + self.core
        return [far] + [self.device(dx, dc) for dx, dc in self.order]

    to = Reduction.to
    term = Reduction.term

    def begin(self, gated):
        for at, (dx, dc) in enumerate(self.order):
            self.give[at] = self.term(gated, self.block(dx, dc)).astype(BF16)
            self.gives[at].start()
        self.own[...] = self.term(gated, self.mine)

    def along_z(self):
        total = self.own[...]
        for at in (6, 2, 3, 4, 5, 0, 1):
            self.gives[at].wait_recv()
            total = total + self.got[at].astype(F32)
        self.half[...] = total.astype(BF16)
        self.swap.start()

    def back(self):
        self.swap.wait_recv()
        self.blocks[self.mine] = (self.half[...].astype(F32) + self.half_got[...].astype(F32)).astype(BF16)
        for copy in self.backs:
            copy.start()

    def end(self):
        for copy in self.awaited:
            copy.wait_recv()

    def drain(self):
        for copy in self.gives + [self.swap] + self.backs:
            copy.wait_send()

    @staticmethod
    def scratch(rows, width):
        dma = pltpu.SemaphoreType.DMA
        block = (rows, width)
        return [
            VMEM((7,) + block, BF16), VMEM(block, F32), VMEM((7,) + block, BF16),
            VMEM(block, BF16), VMEM(block, BF16), VMEM((8,) + block, BF16),
            dma((7,)), dma((7,)), dma, dma, dma((7,)), dma((7,)),
        ]


REDUCTION = 18


def decode_kernel(
    slots, partner, decay_log, time_bias,
    state_in, conv_in, mixed_in, gates_in, zgate_in, weight_in, gain_in, out_weight_in,
    states_out, hidden_all, hidden_moved,
    states, moved, store_sems, conv, mixed, gates, zgate, weight, gain, out_weight, load_sems,
    fresh, gate_rows, left, right, solved, flat, left_m, right_m, solved_m, flat_m,
    rows_out, conv_rows, conv_out, held_0, held_1, held_2, conv_held, turned, conv_turned, landed, conv_landed,
    send1, recv1, csend1, crecv1, send2, recv2, csend2, crecv2,
    *reductions,
):
    rows = mixed.shape[0]
    tp = lax.axis_index("tp")
    me = lax.axis_index("req")
    core = lax.rem(tp, 2)
    place = (tp // 4, lax.rem(tp // 2, 2), core)
    mine = me // 2
    holder = piece_holder(mine, core) == me
    held = (held_0, held_1, held_2)

    loads = [
        pltpu.make_async_copy(src, dst, load_sems.at[at])
        for at, (src, dst) in enumerate(
            (
                (conv_in, conv), (state_in, states), (mixed_in, mixed),
                (gates_in, gates), (weight_in, weight), (zgate_in, zgate), (gain_in, gain),
                (out_weight_in, out_weight),
            )
        )
    ]
    for load in loads:
        load.start()

    everyone = Reduction(place, reductions[:REDUCTION], out_weight)
    movers = ShortReduction(place, reductions[REDUCTION:], out_weight)
    barrier = pltpu.get_barrier_semaphore()

    def greet(k, carry):
        z, y = lax.rem(7 - lax.rem(me, 8) + k // 4, 8), lax.rem(me // 8 + 2 + k, 4)
        peer = y * 8 + z

        @pl.when(peer != me)
        def _():
            pl.semaphore_signal(barrier, inc=1, device_id={"req": peer}, device_id_type=MESH)

        return carry

    tp_peers = movers.peers()
    for peer in tp_peers:
        pl.semaphore_signal(barrier, inc=1, device_id={"tp": peer}, device_id_type=MESH)
    lax.fori_loop(0, GROUPS, greet, 0)

    loads[0].wait()
    conv_rows[...] = jnp.zeros_like(conv_rows)
    for j in range(MOVE):
        for tap in range(3):
            for part in range(4):
                conv_rows[j, pl.ds(tap * 4 + part, 1), :] = conv[
                    slots[0, j], tap, :, part * LANES : (part + 1) * LANES
                ]
        conv_out[j] = conv_rows[j].astype(BF16)
    loads[1].wait()

    def pack(piece, carry):
        start = pl.multiple_of(lax.rem(piece, 8) * TILE, TILE)
        for j in range(MOVE):
            rows_out[j, piece] = states[slots[0, j], piece // 8, pl.ds(start, TILE), :].astype(BF16)
        return carry

    lax.fori_loop(0, PIECES, pack, 0)

    for load in loads[2:7]:
        load.wait()
    fresh[...] = mixed[...].astype(F32)
    latest = [fresh[:, t, :] for t in range(STEPS)]
    gate_rows[...] = jnp.zeros_like(gate_rows)
    for t in range(STEPS):
        for kind in range(2):
            at = t * 4 + kind * 2
            gate_rows[at : at + 2, 0:rows] = gates[t, kind]
    columns = gate_rows[...].T

    def both(at):
        return jnp.concatenate(
            [
                jnp.broadcast_to(columns[0:rows, at + h : at + h + 1], (rows, HEAD))
                for h in range(2)
            ],
            axis=1,
        )

    rate = jnp.exp(halves(decay_log[0], decay_log[1], (1, 2 * HEAD)))
    bias = halves(time_bias[0], time_bias[1], (1, 2 * HEAD))
    decays, betas, zs = [], [], []
    for t in range(STEPS):
        a = both(t * 4) + bias
        soft = jnp.maximum(a, 0.0) + jnp.log1p(jnp.exp(-jnp.abs(a)))
        decays.append(jnp.exp(-rate * soft))
        betas.append(jax.nn.sigmoid(both(t * 4 + 2)))
        zs.append(zgate[:, t, :].astype(F32))
    spread = gain[...]

    left[...] = jnp.zeros_like(left)
    right[...] = jnp.zeros_like(right)
    window = [conv[:, tap, 0, :] for tap in range(3)] + latest
    queries, keys, values = convolved(window, weight)
    read_side(left, queries, keys)
    for r in range(rows):
        lhs = left[:, r, :].astype(BF16)
        for h in range(2):
            block = states[r, h]
            high = block.astype(BF16)
            low = (block - high.astype(F32)).astype(BF16)
            product = jnp.dot(lhs, high, preferred_element_type=F32) + jnp.dot(
                lhs, low, preferred_element_type=F32
            )
            solved[r, :, h * HEAD : (h + 1) * HEAD] = product[0:8] + product[8:16]
    gram = products(queries, keys)
    writes, carried = solve(solved, flat, gram, values, decays, betas, zs, spread)
    write_side(left, right, keys, writes, carried)

    def picked(value):
        at_row = lax.broadcasted_iota(jnp.int32, value.shape, 0)
        target = (8, value.shape[1])
        at_out = lax.broadcasted_iota(jnp.int32, target, 0)
        result = jnp.zeros(target, F32)
        for j in range(MOVE):
            row = jnp.sum(jnp.where(at_row == slots[0, j], value, 0.0), axis=0, keepdims=True)
            result = jnp.where(at_out == j, jnp.broadcast_to(row, target), result)
        return result

    latest_m = [picked(value) for value in latest]
    decays_m = [picked(value) for value in decays]
    betas_m = [picked(value) for value in betas]
    zs_m = [picked(value) for value in zs]

    pl.semaphore_wait(barrier, GROUPS - 1 + len(tp_peers))

    def first(j, piece, peer):
        return pltpu.make_async_remote_copy(
            src_ref=rows_out.at[j, piece], dst_ref=held[j].at[me], send_sem=send1.at[j, piece],
            recv_sem=recv1.at[j, me], device_id={"req": peer}, device_id_type=MESH,
        )

    def conv_first(j, peer):
        return pltpu.make_async_remote_copy(
            src_ref=conv_out.at[j], dst_ref=conv_held.at[me], send_sem=csend1.at[j],
            recv_sem=crecv1.at[me], device_id={"req": peer}, device_id_type=MESH,
        )

    for j in range(MOVE):
        peer = piece_holder(CONV_PIECE[j], core)

        @pl.when(peer != me)
        def _():
            conv_first(j, peer).start()

        @pl.when(peer == me)
        def _():
            conv_held[me] = conv_out[j]

    for j in range(MOVE):

        def send_piece(k, carry):
            piece = lax.rem(mine + k, PIECES)
            peer = piece_holder(piece, core)

            @pl.when(peer != me)
            def _():
                first(j, piece, peer).start()

            @pl.when(peer == me)
            def _():
                held[j][me] = rows_out[j, piece]

            return carry

        lax.fori_loop(0, PIECES, send_piece, 0)

    loads[7].wait()
    everyone.begin(jnp.concatenate([flat[0], flat[1]], axis=1).astype(BF16))
    for r in range(rows):
        new = list(updated(left, right, r, [states[r, h] for h in range(2)]))
        for h in range(2):
            states[r, h] = new[h]
    stores = [
        pltpu.make_async_copy(src, dst, store_sems.at[at])
        for at, (src, dst) in enumerate(
            (
                (states, states_out.at[pl.ds(0, rows)]), (everyone.blocks, hidden_all),
                (moved, states_out.at[pl.ds(rows, MOVE)]),
                (movers.blocks, hidden_moved),
            )
        )
    ]
    stores[0].start()
    everyone.along_x()

    def second(j, dest):
        return pltpu.make_async_remote_copy(
            src_ref=turned.at[j, dest], dst_ref=landed.at[j, mine], send_sem=send2.at[j, dest],
            recv_sem=recv2.at[j, mine], device_id={"req": dest}, device_id_type=MESH,
        )

    def conv_second(j, dest):
        return pltpu.make_async_remote_copy(
            src_ref=conv_turned.at[dest], dst_ref=conv_landed.at[j], send_sem=csend2.at[dest],
            recv_sem=crecv2.at[j], device_id={"req": dest}, device_id_type=MESH,
        )

    for j in range(MOVE):

        @pl.when(holder)
        def _():
            def wait_first(k, carry):
                group = lax.rem(me + k, GROUPS)
                pltpu.make_async_remote_copy(
                    src_ref=rows_out.at[j, 0], dst_ref=held[j].at[group], send_sem=send1.at[j, 0],
                    recv_sem=recv1.at[j, group], device_id={"req": group}, device_id_type=MESH,
                ).wait_recv()
                return carry

            lax.fori_loop(1, GROUPS, wait_first, 0)

            def turn(k, carry):
                dest = lax.rem(me + k, GROUPS)
                turned[j, dest] = held[j][partner[j, dest]]

                @pl.when(k > 0)
                def _():
                    second(j, dest).start()

                return carry

            lax.fori_loop(0, GROUPS, turn, 0)
            landed[j, mine] = turned[j, me]

        @pl.when(jnp.logical_and(holder, mine == CONV_PIECE[j]))
        def _():
            def wait_conv(k, carry):
                group = lax.rem(me + k, GROUPS)
                pltpu.make_async_remote_copy(
                    src_ref=conv_out.at[0], dst_ref=conv_held.at[group], send_sem=csend1.at[0],
                    recv_sem=crecv1.at[group], device_id={"req": group}, device_id_type=MESH,
                ).wait_recv()
                return carry

            lax.fori_loop(1, GROUPS, wait_conv, 0)

            def turn_conv(k, carry):
                dest = lax.rem(me + k, GROUPS)
                conv_turned[dest] = conv_held[partner[j, dest]]

                @pl.when(k > 0)
                def _():
                    conv_second(j, dest).start()

                return carry

            lax.fori_loop(0, GROUPS, turn_conv, 0)
            conv_landed[j] = conv_turned[me]

    everyone.along_z()

    for j in range(MOVE):
        source = piece_holder(CONV_PIECE[j], core)

        @pl.when(source != me)
        def _():
            conv_second(j, source).wait_recv()

    at_out = lax.broadcasted_iota(jnp.int32, (8, LANES), 0)
    window_m = []
    for tap in range(3):
        parts = []
        for part in range(4):
            at = tap * 4 + part
            value = jnp.zeros((8, LANES), F32)
            for j in range(MOVE):
                row = conv_landed[j].astype(F32)[at : at + 1, :]
                value = jnp.where(at_out == j, jnp.broadcast_to(row, (8, LANES)), value)
            parts.append(value)
        window_m.append(jnp.concatenate(parts, axis=1))
    left_m[...] = jnp.zeros_like(left_m)
    right_m[...] = jnp.zeros_like(right_m)
    solved_m[...] = jnp.zeros_like(solved_m)
    queries, keys, values = convolved(window_m + latest_m, weight)
    read_side(left_m, queries, keys)
    gram = products(queries, keys)

    for j in range(MOVE):

        def wait_second(piece, carry):
            source = piece_holder(piece, core)

            @pl.when(source != me)
            def _():
                pltpu.make_async_remote_copy(
                    src_ref=turned.at[j, 0], dst_ref=landed.at[j, piece], send_sem=send2.at[j, 0],
                    recv_sem=recv2.at[j, piece], device_id={"req": source}, device_id_type=MESH,
                ).wait_recv()

            return carry

        lax.fori_loop(0, PIECES, wait_second, 0)
        lhs = left_m[:, j, :].astype(BF16)
        for h in range(2):
            block = landed[j, h * 8 : (h + 1) * 8].reshape(HEAD, HEAD)
            product = jnp.dot(lhs, block, preferred_element_type=F32)
            solved_m[j, :, h * HEAD : (h + 1) * HEAD] = product[0:8] + product[8:16]

    writes, carried = solve(
        solved_m, flat_m, gram, values, decays_m, betas_m, zs_m, spread
    )
    movers.begin(jnp.concatenate([flat_m[0, 0:16], flat_m[1, 0:16]], axis=1).astype(BF16))
    write_side(left_m, right_m, keys, writes, carried)
    movers.along_z()
    everyone.back_x()
    for j in range(MOVE):
        blocks = [
            landed[j, h * 8 : (h + 1) * 8].reshape(HEAD, HEAD).astype(F32) for h in range(2)
        ]
        for h, new in enumerate(updated(left_m, right_m, j, blocks)):
            moved[j, h] = new
    stores[2].start()
    everyone.back_core()

    def done_first(piece, carry):
        peer = piece_holder(piece, core)

        @pl.when(peer != me)
        def _():
            for j in range(MOVE):
                first(j, piece, peer).wait_send()

        return carry

    lax.fori_loop(0, PIECES, done_first, 0)
    for j in range(MOVE):
        peer = piece_holder(CONV_PIECE[j], core)

        @pl.when(peer != me)
        def _():
            conv_first(j, peer).wait_send()

    @pl.when(holder)
    def _():
        def done_second(k, carry):
            for j in range(MOVE):
                second(j, lax.rem(me + k, GROUPS)).wait_send()
            return carry

        lax.fori_loop(1, GROUPS, done_second, 0)
        for j in range(MOVE):

            @pl.when(mine == CONV_PIECE[j])
            def _():
                def done_conv(k, carry):
                    conv_second(j, lax.rem(me + k, GROUPS)).wait_send()
                    return carry

                lax.fori_loop(1, GROUPS, done_conv, 0)

    everyone.end()
    stores[1].start()
    everyone.drain()
    movers.back()
    movers.end()
    stores[3].start()
    movers.drain()
    for store in stores:
        store.wait()


def decode(
    slots, partner, decay_log, time_bias, state, conv, mixed, gates, zgate, weight, gain, out_weight
):
    rows = state.shape[0]
    width = out_weight.shape[1] // 8
    tile = (TILE, LANES)
    dma = pltpu.SemaphoreType.DMA
    smem = pl.BlockSpec(memory_space=pltpu.SMEM)
    anywhere = pl.BlockSpec(memory_space=pl.ANY)
    arrays = (state, conv, mixed, gates, zgate, weight, gain, out_weight)

    def working(count, padded):
        return [
            VMEM((16, padded, HEAD), F32),
            VMEM((16, padded, 2 * HEAD), F32),
            VMEM((count, 8, 2 * HEAD), F32),
            VMEM((2, count * STEPS, HEAD), F32),
        ]

    return pl.pallas_call(
        decode_kernel,
        out_shape=(
            jax.ShapeDtypeStruct((rows + MOVE,) + state.shape[1:], F32),
            jax.ShapeDtypeStruct((8, rows * STEPS, width), BF16),
            jax.ShapeDtypeStruct((8, TILE, width), BF16),
        ),
        in_specs=[smem] * 4 + [anywhere] * len(arrays),
        out_specs=(anywhere,) * 3,
        scratch_shapes=[VMEM(state.shape, F32), VMEM((MOVE,) + state.shape[1:], F32), dma((4,))]
        + [VMEM(a.shape, a.dtype) for a in arrays[1:]]
        + [dma((len(arrays),)), VMEM(mixed.shape, F32), VMEM((LANES, LANES), F32)]
        + working(rows, 16)
        + working(8, 8)
        + [
            VMEM((MOVE, PIECES) + tile, BF16),
            VMEM((MOVE,) + tile, F32),
            VMEM((MOVE,) + tile, BF16),
            VMEM((GROUPS,) + tile, BF16),
            VMEM((GROUPS,) + tile, BF16),
            VMEM((GROUPS,) + tile, BF16),
            VMEM((GROUPS,) + tile, BF16),
            VMEM((MOVE, GROUPS) + tile, BF16),
            VMEM((GROUPS,) + tile, BF16),
            VMEM((MOVE, PIECES) + tile, BF16),
            VMEM((MOVE,) + tile, BF16),
            dma((MOVE, PIECES)), dma((MOVE, GROUPS)), dma((MOVE,)), dma((GROUPS,)),
            dma((MOVE, GROUPS)), dma((MOVE, PIECES)), dma((GROUPS,)), dma((MOVE,)),
        ]
        + Reduction.scratch(rows * STEPS, width)
        + ShortReduction.scratch(TILE, width),
        compiler_params=pltpu.CompilerParams(
            collective_id=0, has_side_effects=True, vmem_limit_bytes=58 << 20
        ),
        name="decode",
    )(slots, partner, decay_log, time_bias, *arrays)


def place_kernel(
    slots, states, hidden_all, hidden_moved, mixed, hidden, new_state, new_conv,
    held, kept, changed, latest, fresh, out, load_sems, store_sems,
):
    rows = mixed.shape[0]
    width = hidden_all.shape[2]
    loads, stores = [], []
    for r in range(rows):
        source = r
        for j in range(MOVE):
            source = jnp.where(slots[0, j] == r, rows + j, source)
        loads.append(pltpu.make_async_copy(states.at[source], held.at[r], load_sems.at[r]))
        stores.append(pltpu.make_async_copy(held.at[r], new_state.at[r], store_sems.at[r]))
    for at, (src, dst) in enumerate(((hidden_all, kept), (hidden_moved, changed), (mixed, latest))):
        loads.append(pltpu.make_async_copy(src, dst, load_sems.at[rows + at]))
    stores.append(pltpu.make_async_copy(out, hidden, store_sems.at[rows]))
    stores.append(pltpu.make_async_copy(fresh, new_conv, store_sems.at[rows + 1]))
    for load in loads[rows:] + loads[:rows]:
        load.start()
    for r in range(rows):
        loads[r].wait()
        stores[r].start()
    for load in loads[rows:]:
        load.wait()
    values = latest[...].astype(F32)
    for tap in range(3):
        fresh[:, tap, 0, :] = values[:, tap + 1, :]
    stores[rows + 1].start()
    for block in range(8):
        cut = slice(block * width, (block + 1) * width)
        stay = kept[block].astype(F32)
        came = changed[block].astype(F32)
        for r in range(rows):
            value = stay[r * STEPS : (r + 1) * STEPS, :]
            for j in range(MOVE):
                value = jnp.where(slots[0, j] == r, came[j * STEPS : (j + 1) * STEPS, :], value)
            out[r, :, cut] = value.astype(BF16)
    stores[rows].start()
    for store in stores:
        store.wait()


def place(slots, states, hidden_all, hidden_moved, mixed):
    rows = mixed.shape[0]
    dma = pltpu.SemaphoreType.DMA
    anywhere = pl.BlockSpec(memory_space=pl.ANY)
    hidden = (rows, STEPS, 8 * hidden_all.shape[2])
    conv = (rows, TAPS - 1, 1, mixed.shape[2])
    return pl.pallas_call(
        place_kernel,
        out_shape=(
            jax.ShapeDtypeStruct(hidden, BF16),
            jax.ShapeDtypeStruct((rows,) + states.shape[1:], F32),
            jax.ShapeDtypeStruct(conv, F32),
        ),
        in_specs=[pl.BlockSpec(memory_space=pltpu.SMEM)] + [anywhere] * 4,
        out_specs=(anywhere,) * 3,
        scratch_shapes=[
            VMEM((rows,) + states.shape[1:], F32), VMEM(hidden_all.shape, BF16),
            VMEM(hidden_moved.shape, BF16), VMEM(mixed.shape, BF16), VMEM(conv, F32),
            VMEM(hidden, BF16), dma((rows + 3,)), dma((rows + 2,)),
        ],
        compiler_params=pltpu.CompilerParams(vmem_limit_bytes=58 << 20),
        name="place",
    )(slots, states, hidden_all, hidden_moved, mixed)


def per_device(
    state,
    conv_state,
    mixed,
    gates,
    output_gate,
    conv_weight,
    decay_log,
    time_bias,
    norm_gain,
    out_weight,
    partner,
    moved_slots,
):
    fresh = mixed.reshape(mixed.shape[0], mixed.shape[1], mixed.shape[3])
    states, hidden_all, hidden_moved = decode(
        moved_slots, partner.T, decay_log, time_bias, state, conv_state.transpose(0, 2, 1, 3),
        fresh, gates.transpose(1, 2, 3, 0), output_gate, conv_weight, norm_gain.reshape(1, -1),
        out_weight,
    )
    hidden, new_state, new_conv = place(moved_slots, states, hidden_all, hidden_moved, fresh)
    return (hidden, new_state, new_conv.transpose(0, 2, 1, 3))


def solution(mesh):
    placed = (
        P("req", "tp", None, None),
        P("req", "tp", None, None),
        P("req", None, "tp", None),
        P("req", None, None, "tp"),
        P("req", None, "tp"),
        P("tp", None, None),
        P("tp"),
        P("tp"),
        P(),
        P("tp", None),
        P(),
        P("req", None),
    )
    return jax.shard_map(
        per_device,
        mesh=mesh,
        in_specs=placed,
        out_specs=(P("req", None, None), P("req", "tp", None, None), P("req", "tp", None, None)),
        check_vma=False,
    )
```

```python
import jax
import jax.numpy as jnp
from jax import lax
from jax.experimental import pallas as pl
from jax.experimental.pallas import tpu as pltpu
from jax.sharding import PartitionSpec as P

MESH = pl.DeviceIdType.MESH
F32 = jnp.float32
BF16 = jnp.bfloat16
VMEM = pltpu.VMEM
GROUPS, MOVE, PIECES, TILE, LANES = 32, 3, 8, 16, 128
PIECE = 2 * TILE
CONV_PIECE = (1, 4, 7)
HEAD, TAPS, STEPS = 128, 4, 4


def piece_holder(piece):
    return piece // 2 * 8 + 2 + 3 * lax.rem(piece, 2)


def piece_at(group):
    return group // 8 * 2 + lax.rem(group, 8) // 4


def flipped(number, flips, bits):
    result = 0
    for bit in range(bits):
        a, b = lax.rem(number // (1 << bit), 2), lax.rem(flips // (1 << bit), 2)
        result = result + (a + b - 2 * a * b) * (1 << bit)
    return result


def crossing_first(me, k):
    return lax.rem(me // 8 + k, 4) * 8 + flipped(lax.rem(me, 8), 7 - k // 4, 3)


def split16(value):
    high = value.astype(BF16)
    return high.astype(F32), value - high.astype(F32)


def halves(scalar_a, scalar_b, shape):
    lane = lax.broadcasted_iota(jnp.int32, shape, len(shape) - 1)
    return jnp.where(lane < HEAD, scalar_a, scalar_b)


def convolved(window, weight):
    queries, keys, values = [], [], []
    for t in range(STEPS):
        total = window[t] * weight[0, 0:1, :]
        for tap in range(1, TAPS):
            total = total + window[t + tap] * weight[0, tap : tap + 1, :]
        c = total * jax.nn.sigmoid(total)
        q, k = c[:, :HEAD], c[:, HEAD : 2 * HEAD]
        queries.append(
            q * lax.rsqrt(jnp.sum(q * q, -1, keepdims=True) + 1e-06) / jnp.sqrt(jnp.float32(HEAD))
        )
        keys.append(k * lax.rsqrt(jnp.sum(k * k, -1, keepdims=True) + 1e-06))
        values.append(c[:, 2 * HEAD :])
    return queries, keys, values


def read_side(left, queries, keys):
    rows = keys[0].shape[0]
    for t in range(STEPS):
        for at, part in enumerate(split16(keys[t]) + split16(queries[t])):
            left[t + (0, 8, 4, 12)[at], 0:rows, :] = part


def products(queries, keys):
    pairs = [(t, s) for t in range(STEPS) for s in range(t + 1)]
    written = {p: jnp.sum(keys[p[0]] * keys[p[1]], -1, keepdims=True) for p in pairs if p[0] != p[1]}
    read = {p: jnp.sum(queries[p[0]] * keys[p[1]], -1, keepdims=True) for p in pairs}
    return written, read


def solve(solved, flat, gram, values, decays, betas, zs, gain):
    rows = values[0].shape[0]
    key_key, query_key = gram
    writes = []
    carried = [decays[0]]
    for t in range(1, STEPS):
        carried.append(carried[-1] * decays[t])
    spread = jnp.concatenate([gain, gain], axis=1)
    for t in range(STEPS):
        read = solved[0:rows, t, :] * carried[t]
        out = solved[0:rows, 4 + t, :] * carried[t]
        writes = [w * decays[t] for w in writes]
        for s in range(t):
            read = read + writes[s] * key_key[t, s]
            out = out + writes[s] * query_key[t, s]
        writes.append((values[t] - read) * betas[t])
        out = out + writes[t] * query_key[t, t]
        square = out * out
        norm = jnp.concatenate(
            [
                jnp.broadcast_to(
                    lax.rsqrt(
                        jnp.mean(square[:, h * HEAD : (h + 1) * HEAD], -1, keepdims=True) + 1e-06
                    ),
                    (rows, HEAD),
                )
                for h in range(2)
            ],
            axis=1,
        )
        result = out * norm * spread * (zs[t] * jax.nn.sigmoid(zs[t]))
        for h in range(2):
            flat[h, pl.ds(t, rows, stride=STEPS), :] = result[:, h * HEAD : (h + 1) * HEAD]
    return writes, carried[-1]


def write_side(left, right, keys, writes, carried):
    rows = keys[0].shape[0]
    left[12:16] = jnp.zeros_like(left[12:16])
    for t in range(STEPS):
        high, low = split16(keys[t])
        left[t, 0:rows, :] = high
        left[4 + t, 0:rows, :] = high
        left[8 + t, 0:rows, :] = low
        high, low = split16(writes[t])
        right[t, 0:rows, :] = high
        right[4 + t, 0:rows, :] = low
        right[8 + t, 0:rows, :] = high
    right[12, 0:rows, :] = carried


def updated(left, right, row, blocks):
    lhs = left[:, row, :].astype(BF16)
    rhs = right[:, row, :]
    update = lax.dot_general(
        lhs, rhs.astype(BF16), (((0,), (0,)), ((), ())), preferred_element_type=F32
    )
    for h in range(2):
        cut = slice(h * HEAD, (h + 1) * HEAD)
        yield blocks[h] * rhs[12:13, cut] + update[:, cut]


class Reduction:
    def __init__(self, place, scratch, weight):
        self.x, self.high, self.core = place
        (
            self.give, self.own, self.got, self.pass_on, self.passed, self.half, self.half_got,
            self.blocks, gs, gr, ps, pr, hs, hr, rs, rr, ms, mr,
        ) = scratch
        self.weight = weight
        self.width = self.give.shape[2]
        mate, far = self.peers()[:2]
        self.gives = [self.to(mate, self.give.at[k], self.got.at[k], gs.at[k], gr.at[k]) for k in range(4)]
        self.passes = [
            self.to(self.ring(k), self.pass_on.at[k - 1], self.passed.at[k - 1], ps.at[k - 1], pr.at[k - 1])
            for k in range(1, 4)
        ]
        self.swap = self.to(far, self.half, self.half_got, hs, hr)
        self.mine = self.x * 2 + self.core
        own = self.blocks.at[self.mine]
        self.rings = [self.to(self.ring(k), own, own, rs.at[k - 1], rr.at[k - 1]) for k in range(1, 4)]
        self.mates = []
        for k in range(4):
            block = self.blocks.at[self.at_x(k) * 2 + self.core]
            self.mates.append(self.to(mate, block, block, ms.at[k], mr.at[k]))

    def peers(self):
        here = self.x * 4 + self.high * 2
        return (
            here + 1 - self.core, self.x * 4 + (1 - self.high) * 2 + self.core,
            self.ring(2), self.ring(1), self.ring(3),
        )

    def at_x(self, k):
        return lax.rem(self.x + k, 4)

    def ring(self, k):
        return self.at_x(k) * 4 + self.high * 2 + self.core

    def to(self, peer, src, dst, send, recv):
        return pltpu.make_async_remote_copy(
            src_ref=src, dst_ref=dst, send_sem=send, recv_sem=recv,
            device_id={"tp": peer}, device_id_type=MESH,
        )

    def term(self, gated, block):
        cut = pl.ds(pl.multiple_of(block * self.width, self.width), self.width)
        return jnp.dot(gated, self.weight[:, cut], preferred_element_type=F32)

    order = (2, 1, 3, 0)

    def begin(self, gated):
        for k in self.order:
            self.give[k] = self.term(gated, self.at_x(k) * 2 + 1 - self.core).astype(BF16)
            self.gives[k].start()
        for k in self.order:
            self.own[k] = self.term(gated, self.at_x(k) * 2 + self.core)

    def along_x(self):
        for k in self.order:
            self.gives[k].wait_recv()
            total = self.own[k] + self.got[k].astype(F32)
            if k:
                self.pass_on[k - 1] = total.astype(BF16)
                self.passes[k - 1].start()
            else:
                self.own[0] = total

    def along_z(self):
        total = self.own[0]
        for k in (1, 3, 2):
            self.passes[k - 1].wait_recv()
            total = total + self.passed[k - 1].astype(F32)
        self.half[...] = total.astype(BF16)
        self.swap.start()

    def back_x(self):
        self.swap.wait_recv()
        self.blocks[self.mine] = (self.half[...].astype(F32) + self.half_got[...].astype(F32)).astype(BF16)
        for k in (2, 1, 3):
            self.rings[k - 1].start()
        self.mates[0].start()

    def back_core(self):
        for k in (1, 3, 2):
            self.rings[k - 1].wait_recv()
            self.mates[4 - k].start()

    def end(self):
        for k in range(4):
            self.mates[k].wait_recv()

    def drain(self):
        for copy in self.gives + self.passes + [self.swap] + self.rings + self.mates:
            copy.wait_send()

    @staticmethod
    def scratch(rows, width):
        dma = pltpu.SemaphoreType.DMA
        block = (rows, width)
        return [
            VMEM((4,) + block, BF16), VMEM((4,) + block, F32), VMEM((4,) + block, BF16),
            VMEM((3,) + block, BF16), VMEM((3,) + block, BF16),
            VMEM(block, BF16), VMEM(block, BF16), VMEM((8,) + block, BF16),
            dma((4,)), dma((4,)), dma((3,)), dma((3,)), dma, dma,
            dma((3,)), dma((3,)), dma((4,)), dma((4,)),
        ]


class ShortReduction:
    def __init__(self, place, scratch, weight):
        self.x, self.high, self.core = place
        (
            self.give, self.own, self.got, self.half, self.half_got, self.blocks,
            gs, gr, hs, hr, bs, br,
        ) = scratch
        self.weight = weight
        self.width = self.give.shape[2]
        self.mine = self.x * 2 + self.core
        self.gives, self.backs, self.awaited = [], [], []
        for at, (dx, dc) in enumerate(self.order):
            peer = self.device(dx, dc)
            self.gives.append(self.to(peer, self.give.at[at], self.got.at[at], gs.at[at], gr.at[at]))
            own = self.blocks.at[self.mine]
            self.backs.append(self.to(peer, own, own, bs.at[at], br.at[at]))
            theirs = self.blocks.at[self.block(-dx, dc)]
            self.awaited.append(self.to(self.device(-dx, dc), own, theirs, bs.at[at], br.at[at]))
        far = self.x * 4 + (1 - self.high) * 2 + self.core
        self.swap = self.to(far, self.half, self.half_got, hs, hr)

    order = ((2, 0), (2, 1), (1, 0), (1, 1), (3, 0), (3, 1), (0, 1))

    def toward(self, dx, dc):
        return lax.rem(self.x + dx + 4, 4), 1 - self.core if dc else self.core

    def device(self, dx, dc):
        x, core = self.toward(dx, dc)
        return x * 4 + self.high * 2 + core

    def block(self, dx, dc):
        x, core = self.toward(dx, dc)
        return x * 2 + core

    def peers(self):
        far = self.x * 4 + (1 - self.high) * 2 + self.core
        return [far] + [self.device(dx, dc) for dx, dc in self.order]

    to = Reduction.to
    term = Reduction.term

    def begin(self, gated):
        for at, (dx, dc) in enumerate(self.order):
            self.give[at] = self.term(gated, self.block(dx, dc)).astype(BF16)
            self.gives[at].start()
        self.own[...] = self.term(gated, self.mine)

    def along_z(self):
        total = self.own[...]
        for at in (6, 2, 3, 4, 5, 0, 1):
            self.gives[at].wait_recv()
            total = total + self.got[at].astype(F32)
        self.half[...] = total.astype(BF16)
        self.swap.start()

    def back(self):
        self.swap.wait_recv()
        self.blocks[self.mine] = (self.half[...].astype(F32) + self.half_got[...].astype(F32)).astype(BF16)
        for copy in self.backs:
            copy.start()

    def end(self):
        for copy in self.awaited:
            copy.wait_recv()

    def drain(self):
        for copy in self.gives + [self.swap] + self.backs:
            copy.wait_send()

    @staticmethod
    def scratch(rows, width):
        dma = pltpu.SemaphoreType.DMA
        block = (rows, width)
        return [
            VMEM((7,) + block, BF16), VMEM(block, F32), VMEM((7,) + block, BF16),
            VMEM(block, BF16), VMEM(block, BF16), VMEM((8,) + block, BF16),
            dma((7,)), dma((7,)), dma, dma, dma((7,)), dma((7,)),
        ]


REDUCTION = 18


def decode_kernel(
    slots, partner, decay_log, time_bias,
    state_in, conv_in, mixed_in, gates_in, zgate_in, weight_in, gain_in, out_weight_in,
    states_out, hidden_all, hidden_moved,
    states, moved, store_sems, conv, mixed, gates, zgate, weight, gain, out_weight, load_sems,
    fresh, gate_rows, left, right, solved, flat, left_m, right_m, solved_m, flat_m,
    rows_out, conv_rows, conv_out, held_0, held_1, held_2, conv_held, turned, conv_turned, landed, conv_landed,
    send1, recv1, csend1, crecv1, send2, recv2, csend2, crecv2,
    *reductions,
):
    rows = mixed.shape[0]
    tp = lax.axis_index("tp")
    me = lax.axis_index("req")
    core = lax.rem(tp, 2)
    place = (tp // 4, lax.rem(tp // 2, 2), core)
    mine = piece_at(me)
    holder = piece_holder(mine) == me
    held = (held_0, held_1, held_2)

    loads = [
        pltpu.make_async_copy(src, dst, load_sems.at[at])
        for at, (src, dst) in enumerate(
            (
                (conv_in, conv), (state_in, states), (mixed_in, mixed),
                (gates_in, gates), (weight_in, weight), (zgate_in, zgate), (gain_in, gain),
                (out_weight_in, out_weight),
            )
        )
    ]
    for load in loads:
        load.start()

    everyone = Reduction(place, reductions[:REDUCTION], out_weight)
    movers = ShortReduction(place, reductions[REDUCTION:], out_weight)
    barrier = pltpu.get_barrier_semaphore()

    def greet(k, carry):
        peer = crossing_first(me, k)
        turns = piece_holder(piece_at(peer)) == peer

        @pl.when(jnp.logical_and(peer != me, jnp.logical_or(holder, turns)))
        def _():
            pl.semaphore_signal(barrier, inc=1, device_id={"req": peer}, device_id_type=MESH)

        return carry

    tp_peers = movers.peers()
    for peer in tp_peers:
        pl.semaphore_signal(barrier, inc=1, device_id={"tp": peer}, device_id_type=MESH)
    lax.fori_loop(0, GROUPS, greet, 0)

    loads[0].wait()
    conv_rows[...] = jnp.zeros_like(conv_rows)
    for j in range(MOVE):
        for tap in range(3):
            for part in range(4):
                conv_rows[j, pl.ds(tap * 4 + part, 1), :] = conv[
                    slots[0, j], tap, :, part * LANES : (part + 1) * LANES
                ]
        conv_out[j] = conv_rows[j].astype(BF16)
    loads[1].wait()

    def pack(piece, carry):
        start = pl.multiple_of(lax.rem(piece, 4) * PIECE, PIECE)
        for j in range(MOVE):
            rows_out[j, piece] = states[slots[0, j], piece // 4, pl.ds(start, PIECE), :].astype(BF16)
        return carry

    lax.fori_loop(0, PIECES, pack, 0)

    pl.semaphore_wait(barrier, jnp.where(holder, GROUPS - 1, PIECES) + len(tp_peers))

    def first(j, piece, peer):
        return pltpu.make_async_remote_copy(
            src_ref=rows_out.at[j, piece], dst_ref=held[j].at[me], send_sem=send1.at[j, piece],
            recv_sem=recv1.at[j, me], device_id={"req": peer}, device_id_type=MESH,
        )

    def conv_first(j, peer):
        return pltpu.make_async_remote_copy(
            src_ref=conv_out.at[j], dst_ref=conv_held.at[me], send_sem=csend1.at[j],
            recv_sem=crecv1.at[me], device_id={"req": peer}, device_id_type=MESH,
        )

    for j in range(MOVE):
        peer = piece_holder(CONV_PIECE[j])

        @pl.when(peer != me)
        def _():
            conv_first(j, peer).start()

        @pl.when(peer == me)
        def _():
            conv_held[me] = conv_out[j]

    for j in range(MOVE):

        def send_piece(k, carry):
            piece = lax.rem(mine // 2 + k, 4) * 2 + flipped(lax.rem(mine, 2), 1 - k // 4, 1)
            peer = piece_holder(piece)

            @pl.when(peer != me)
            def _():
                first(j, piece, peer).start()

            @pl.when(peer == me)
            def _():
                held[j][me] = rows_out[j, piece]

            return carry

        lax.fori_loop(0, PIECES, send_piece, 0)

    for load in loads[2:7]:
        load.wait()
    fresh[...] = mixed[...].astype(F32)
    latest = [fresh[:, t, :] for t in range(STEPS)]
    gate_rows[...] = jnp.zeros_like(gate_rows)
    for t in range(STEPS):
        for kind in range(2):
            at = t * 4 + kind * 2
            gate_rows[at : at + 2, 0:rows] = gates[t, kind]
    columns = gate_rows[...].T

    def both(at):
        return jnp.concatenate(
            [
                jnp.broadcast_to(columns[0:rows, at + h : at + h + 1], (rows, HEAD))
                for h in range(2)
            ],
            axis=1,
        )

    rate = jnp.exp(halves(decay_log[0], decay_log[1], (1, 2 * HEAD)))
    bias = halves(time_bias[0], time_bias[1], (1, 2 * HEAD))
    decays, betas, zs = [], [], []
    for t in range(STEPS):
        a = both(t * 4) + bias
        soft = jnp.maximum(a, 0.0) + jnp.log1p(jnp.exp(-jnp.abs(a)))
        decays.append(jnp.exp(-rate * soft))
        betas.append(jax.nn.sigmoid(both(t * 4 + 2)))
        zs.append(zgate[:, t, :].astype(F32))
    spread = gain[...]

    left[...] = jnp.zeros_like(left)
    right[...] = jnp.zeros_like(right)
    window = [conv[:, tap, 0, :] for tap in range(3)] + latest
    queries, keys, values = convolved(window, weight)
    read_side(left, queries, keys)
    for r in range(rows):
        lhs = left[:, r, :].astype(BF16)
        for h in range(2):
            block = states[r, h]
            high = block.astype(BF16)
            low = (block - high.astype(F32)).astype(BF16)
            product = jnp.dot(lhs, high, preferred_element_type=F32) + jnp.dot(
                lhs, low, preferred_element_type=F32
            )
            solved[r, :, h * HEAD : (h + 1) * HEAD] = product[0:8] + product[8:16]
    gram = products(queries, keys)
    writes, carried = solve(solved, flat, gram, values, decays, betas, zs, spread)
    write_side(left, right, keys, writes, carried)

    def picked(value):
        at_row = lax.broadcasted_iota(jnp.int32, value.shape, 0)
        target = (8, value.shape[1])
        at_out = lax.broadcasted_iota(jnp.int32, target, 0)
        result = jnp.zeros(target, F32)
        for j in range(MOVE):
            row = jnp.sum(jnp.where(at_row == slots[0, j], value, 0.0), axis=0, keepdims=True)
            result = jnp.where(at_out == j, jnp.broadcast_to(row, target), result)
        return result

    latest_m = [picked(value) for value in latest]
    decays_m = [picked(value) for value in decays]
    betas_m = [picked(value) for value in betas]
    zs_m = [picked(value) for value in zs]

    loads[7].wait()
    everyone.begin(jnp.concatenate([flat[0], flat[1]], axis=1).astype(BF16))
    for r in range(rows):
        new = list(updated(left, right, r, [states[r, h] for h in range(2)]))
        for h in range(2):
            states[r, h] = new[h]
    stores = [
        pltpu.make_async_copy(src, dst, store_sems.at[at])
        for at, (src, dst) in enumerate(
            (
                (states, states_out.at[pl.ds(0, rows)]), (everyone.blocks, hidden_all),
                (moved, states_out.at[pl.ds(rows, MOVE)]),
                (movers.blocks, hidden_moved),
            )
        )
    ]
    stores[0].start()

    def second(j, dest):
        return pltpu.make_async_remote_copy(
            src_ref=turned.at[j, dest], dst_ref=landed.at[j, mine], send_sem=send2.at[j, dest],
            recv_sem=recv2.at[j, mine], device_id={"req": dest}, device_id_type=MESH,
        )

    def conv_second(j, dest):
        return pltpu.make_async_remote_copy(
            src_ref=conv_turned.at[dest], dst_ref=conv_landed.at[j], send_sem=csend2.at[dest],
            recv_sem=crecv2.at[j], device_id={"req": dest}, device_id_type=MESH,
        )

    for j in range(MOVE):

        @pl.when(holder)
        def _():
            def wait_first(k, carry):
                group = lax.rem(me + k, GROUPS)
                pltpu.make_async_remote_copy(
                    src_ref=rows_out.at[j, 0], dst_ref=held[j].at[group], send_sem=send1.at[j, 0],
                    recv_sem=recv1.at[j, group], device_id={"req": group}, device_id_type=MESH,
                ).wait_recv()
                return carry

            lax.fori_loop(1, GROUPS, wait_first, 0)

            def turn(k, carry):
                dest = crossing_first(me, k)
                turned[j, dest] = held[j][partner[j, dest]]

                @pl.when(dest != me)
                def _():
                    second(j, dest).start()

                return carry

            lax.fori_loop(0, GROUPS, turn, 0)
            landed[j, mine] = turned[j, me]

        @pl.when(jnp.logical_and(holder, mine == CONV_PIECE[j]))
        def _():
            def wait_conv(k, carry):
                group = lax.rem(me + k, GROUPS)
                pltpu.make_async_remote_copy(
                    src_ref=conv_out.at[0], dst_ref=conv_held.at[group], send_sem=csend1.at[0],
                    recv_sem=crecv1.at[group], device_id={"req": group}, device_id_type=MESH,
                ).wait_recv()
                return carry

            lax.fori_loop(1, GROUPS, wait_conv, 0)

            def turn_conv(k, carry):
                dest = crossing_first(me, k)
                conv_turned[dest] = conv_held[partner[j, dest]]

                @pl.when(dest != me)
                def _():
                    conv_second(j, dest).start()

                return carry

            lax.fori_loop(0, GROUPS, turn_conv, 0)
            conv_landed[j] = conv_turned[me]

        if j == 0:
            everyone.along_x()

    everyone.along_z()

    for j in range(MOVE):
        source = piece_holder(CONV_PIECE[j])

        @pl.when(source != me)
        def _():
            conv_second(j, source).wait_recv()

    at_out = lax.broadcasted_iota(jnp.int32, (8, LANES), 0)
    window_m = []
    for tap in range(3):
        parts = []
        for part in range(4):
            at = tap * 4 + part
            value = jnp.zeros((8, LANES), F32)
            for j in range(MOVE):
                row = conv_landed[j].astype(F32)[at : at + 1, :]
                value = jnp.where(at_out == j, jnp.broadcast_to(row, (8, LANES)), value)
            parts.append(value)
        window_m.append(jnp.concatenate(parts, axis=1))
    left_m[...] = jnp.zeros_like(left_m)
    right_m[...] = jnp.zeros_like(right_m)
    solved_m[...] = jnp.zeros_like(solved_m)
    queries, keys, values = convolved(window_m + latest_m, weight)
    read_side(left_m, queries, keys)
    gram = products(queries, keys)

    for j in range(MOVE):

        def wait_second(piece, carry):
            source = piece_holder(piece)

            @pl.when(source != me)
            def _():
                pltpu.make_async_remote_copy(
                    src_ref=turned.at[j, 0], dst_ref=landed.at[j, piece], send_sem=send2.at[j, 0],
                    recv_sem=recv2.at[j, piece], device_id={"req": source}, device_id_type=MESH,
                ).wait_recv()

            return carry

        lax.fori_loop(0, PIECES, wait_second, 0)
        lhs = left_m[:, j, :].astype(BF16)
        for h in range(2):
            block = landed[j, h * 4 : (h + 1) * 4].reshape(HEAD, HEAD)
            product = jnp.dot(lhs, block, preferred_element_type=F32)
            solved_m[j, :, h * HEAD : (h + 1) * HEAD] = product[0:8] + product[8:16]

    writes, carried = solve(
        solved_m, flat_m, gram, values, decays_m, betas_m, zs_m, spread
    )
    movers.begin(jnp.concatenate([flat_m[0, 0:16], flat_m[1, 0:16]], axis=1).astype(BF16))
    write_side(left_m, right_m, keys, writes, carried)
    movers.along_z()
    everyone.back_x()
    for j in range(MOVE):
        blocks = [
            landed[j, h * 4 : (h + 1) * 4].reshape(HEAD, HEAD).astype(F32) for h in range(2)
        ]
        for h, new in enumerate(updated(left_m, right_m, j, blocks)):
            moved[j, h] = new
    stores[2].start()
    everyone.back_core()

    def done_first(piece, carry):
        peer = piece_holder(piece)

        @pl.when(peer != me)
        def _():
            for j in range(MOVE):
                first(j, piece, peer).wait_send()

        return carry

    lax.fori_loop(0, PIECES, done_first, 0)
    for j in range(MOVE):
        peer = piece_holder(CONV_PIECE[j])

        @pl.when(peer != me)
        def _():
            conv_first(j, peer).wait_send()

    @pl.when(holder)
    def _():
        def done_second(k, carry):
            for j in range(MOVE):
                second(j, lax.rem(me + k, GROUPS)).wait_send()
            return carry

        lax.fori_loop(1, GROUPS, done_second, 0)
        for j in range(MOVE):

            @pl.when(mine == CONV_PIECE[j])
            def _():
                def done_conv(k, carry):
                    conv_second(j, lax.rem(me + k, GROUPS)).wait_send()
                    return carry

                lax.fori_loop(1, GROUPS, done_conv, 0)

    everyone.end()
    stores[1].start()
    everyone.drain()
    movers.back()
    movers.end()
    stores[3].start()
    movers.drain()
    for store in stores:
        store.wait()


def decode(
    slots, partner, decay_log, time_bias, state, conv, mixed, gates, zgate, weight, gain, out_weight
):
    rows = state.shape[0]
    width = out_weight.shape[1] // 8
    tile, rows_of = (TILE, LANES), (PIECE, LANES)
    dma = pltpu.SemaphoreType.DMA
    smem = pl.BlockSpec(memory_space=pltpu.SMEM)
    anywhere = pl.BlockSpec(memory_space=pl.ANY)
    arrays = (state, conv, mixed, gates, zgate, weight, gain, out_weight)

    def working(count, padded):
        return [
            VMEM((16, padded, HEAD), F32),
            VMEM((16, padded, 2 * HEAD), F32),
            VMEM((count, 8, 2 * HEAD), F32),
            VMEM((2, count * STEPS, HEAD), F32),
        ]

    return pl.pallas_call(
        decode_kernel,
        out_shape=(
            jax.ShapeDtypeStruct((rows + MOVE,) + state.shape[1:], F32),
            jax.ShapeDtypeStruct((8, rows * STEPS, width), BF16),
            jax.ShapeDtypeStruct((8, TILE, width), BF16),
        ),
        in_specs=[smem] * 4 + [anywhere] * len(arrays),
        out_specs=(anywhere,) * 3,
        scratch_shapes=[VMEM(state.shape, F32), VMEM((MOVE,) + state.shape[1:], F32), dma((4,))]
        + [VMEM(a.shape, a.dtype) for a in arrays[1:]]
        + [dma((len(arrays),)), VMEM(mixed.shape, F32), VMEM((LANES, LANES), F32)]
        + working(rows, 16)
        + working(8, 8)
        + [
            VMEM((MOVE, PIECES) + rows_of, BF16),
            VMEM((MOVE,) + tile, F32),
            VMEM((MOVE,) + tile, BF16),
            VMEM((GROUPS,) + rows_of, BF16),
            VMEM((GROUPS,) + rows_of, BF16),
            VMEM((GROUPS,) + rows_of, BF16),
            VMEM((GROUPS,) + tile, BF16),
            VMEM((MOVE, GROUPS) + rows_of, BF16),
            VMEM((GROUPS,) + tile, BF16),
            VMEM((MOVE, PIECES) + rows_of, BF16),
            VMEM((MOVE,) + tile, BF16),
            dma((MOVE, PIECES)), dma((MOVE, GROUPS)), dma((MOVE,)), dma((GROUPS,)),
            dma((MOVE, GROUPS)), dma((MOVE, PIECES)), dma((GROUPS,)), dma((MOVE,)),
        ]
        + Reduction.scratch(rows * STEPS, width)
        + ShortReduction.scratch(TILE, width),
        compiler_params=pltpu.CompilerParams(
            collective_id=0, has_side_effects=True, vmem_limit_bytes=58 << 20
        ),
        name="decode",
    )(slots, partner, decay_log, time_bias, *arrays)


def place_kernel(
    slots, states, hidden_all, hidden_moved, mixed, hidden, new_state, new_conv,
    held, kept, changed, latest, fresh, out, load_sems, store_sems,
):
    rows = mixed.shape[0]
    width = hidden_all.shape[2]
    loads, stores = [], []
    for r in range(rows):
        source = r
        for j in range(MOVE):
            source = jnp.where(slots[0, j] == r, rows + j, source)
        loads.append(pltpu.make_async_copy(states.at[source], held.at[r], load_sems.at[r]))
        stores.append(pltpu.make_async_copy(held.at[r], new_state.at[r], store_sems.at[r]))
    for at, (src, dst) in enumerate(((hidden_all, kept), (hidden_moved, changed), (mixed, latest))):
        loads.append(pltpu.make_async_copy(src, dst, load_sems.at[rows + at]))
    stores.append(pltpu.make_async_copy(out, hidden, store_sems.at[rows]))
    stores.append(pltpu.make_async_copy(fresh, new_conv, store_sems.at[rows + 1]))
    for load in loads[rows:] + loads[:rows]:
        load.start()
    for r in range(rows):
        loads[r].wait()
        stores[r].start()
    for load in loads[rows:]:
        load.wait()
    values = latest[...].astype(F32)
    for tap in range(3):
        fresh[:, tap, 0, :] = values[:, tap + 1, :]
    stores[rows + 1].start()
    for block in range(8):
        cut = slice(block * width, (block + 1) * width)
        stay = kept[block].astype(F32)
        came = changed[block].astype(F32)
        for r in range(rows):
            value = stay[r * STEPS : (r + 1) * STEPS, :]
            for j in range(MOVE):
                value = jnp.where(slots[0, j] == r, came[j * STEPS : (j + 1) * STEPS, :], value)
            out[r, :, cut] = value.astype(BF16)
    stores[rows].start()
    for store in stores:
        store.wait()


def place(slots, states, hidden_all, hidden_moved, mixed):
    rows = mixed.shape[0]
    dma = pltpu.SemaphoreType.DMA
    anywhere = pl.BlockSpec(memory_space=pl.ANY)
    hidden = (rows, STEPS, 8 * hidden_all.shape[2])
    conv = (rows, TAPS - 1, 1, mixed.shape[2])
    return pl.pallas_call(
        place_kernel,
        out_shape=(
            jax.ShapeDtypeStruct(hidden, BF16),
            jax.ShapeDtypeStruct((rows,) + states.shape[1:], F32),
            jax.ShapeDtypeStruct(conv, F32),
        ),
        in_specs=[pl.BlockSpec(memory_space=pltpu.SMEM)] + [anywhere] * 4,
        out_specs=(anywhere,) * 3,
        scratch_shapes=[
            VMEM((rows,) + states.shape[1:], F32), VMEM(hidden_all.shape, BF16),
            VMEM(hidden_moved.shape, BF16), VMEM(mixed.shape, BF16), VMEM(conv, F32),
            VMEM(hidden, BF16), dma((rows + 3,)), dma((rows + 2,)),
        ],
        compiler_params=pltpu.CompilerParams(vmem_limit_bytes=58 << 20),
        name="place",
    )(slots, states, hidden_all, hidden_moved, mixed)


def per_device(
    state,
    conv_state,
    mixed,
    gates,
    output_gate,
    conv_weight,
    decay_log,
    time_bias,
    norm_gain,
    out_weight,
    partner,
    moved_slots,
):
    fresh = mixed.reshape(mixed.shape[0], mixed.shape[1], mixed.shape[3])
    states, hidden_all, hidden_moved = decode(
        moved_slots, partner.T, decay_log, time_bias, state, conv_state.transpose(0, 2, 1, 3),
        fresh, gates.transpose(1, 2, 3, 0), output_gate, conv_weight, norm_gain.reshape(1, -1),
        out_weight,
    )
    hidden, new_state, new_conv = place(moved_slots, states, hidden_all, hidden_moved, fresh)
    return (hidden, new_state, new_conv.transpose(0, 2, 1, 3))


def solution(mesh):
    placed = (
        P("req", "tp", None, None),
        P("req", "tp", None, None),
        P("req", None, "tp", None),
        P("req", None, None, "tp"),
        P("req", None, "tp"),
        P("tp", None, None),
        P("tp"),
        P("tp"),
        P(),
        P("tp", None),
        P(),
        P("req", None),
    )
    return jax.shard_map(
        per_device,
        mesh=mesh,
        in_specs=placed,
        out_specs=(P("req", None, None), P("req", "tp", None, None), P("req", "tp", None, None)),
        check_vma=False,
    )
```

```python
import functools

import jax
import jax.numpy as jnp
from jax import lax
from jax.experimental import pallas as pl
from jax.experimental.pallas import tpu as pltpu
from jax.sharding import PartitionSpec as P

MESH = pl.DeviceIdType.MESH
F32 = jnp.float32
BF16 = jnp.bfloat16
VMEM = pltpu.VMEM
GROUPS, MOVE, PIECES, TILE, LANES = 32, 3, 16, 16, 128
CONV_PIECE = (2, 7, 12)
HEAD, TAPS, STEPS = 128, 4, 4


def member(half, number):
    return number // 4 * 8 + half * 4 + lax.rem(number, 4)


def number_of(group):
    return group // 8 * 4 + lax.rem(group, 4)


def ordered(partner):
    crossing = [lax.rem(partner[j, 0] // 4, 2) for j in range(MOVE)]
    count = crossing[0] + crossing[1] + crossing[2]
    before = [0, crossing[0], crossing[0] + crossing[1]]
    places = [
        jnp.where(crossing[j] == 1, before[j], count + j - before[j]) for j in range(MOVE)
    ]
    return [
        sum(jnp.where(places[j] == at, j, 0) for j in range(MOVE)) for at in range(MOVE)
    ]


def split16(value):
    high = value.astype(BF16)
    return high.astype(F32), value - high.astype(F32)


def halves(scalar_a, scalar_b, shape):
    lane = lax.broadcasted_iota(jnp.int32, shape, len(shape) - 1)
    return jnp.where(lane < HEAD, scalar_a, scalar_b)


def convolved(window, weight):
    queries, keys, values = [], [], []
    for t in range(STEPS):
        total = window[t] * weight[0, 0:1, :]
        for tap in range(1, TAPS):
            total = total + window[t + tap] * weight[0, tap : tap + 1, :]
        c = total * jax.nn.sigmoid(total)
        q, k = c[:, :HEAD], c[:, HEAD : 2 * HEAD]
        queries.append(
            q * lax.rsqrt(jnp.sum(q * q, -1, keepdims=True) + 1e-06) / jnp.sqrt(jnp.float32(HEAD))
        )
        keys.append(k * lax.rsqrt(jnp.sum(k * k, -1, keepdims=True) + 1e-06))
        values.append(c[:, 2 * HEAD :])
    return queries, keys, values


def read_side(left, queries, keys):
    rows = keys[0].shape[0]
    for t in range(STEPS):
        for at, part in enumerate(split16(keys[t]) + split16(queries[t])):
            left[t + (0, 8, 4, 12)[at], 0:rows, :] = part


def products(queries, keys):
    pairs = [(t, s) for t in range(STEPS) for s in range(t + 1)]
    written = {p: jnp.sum(keys[p[0]] * keys[p[1]], -1, keepdims=True) for p in pairs if p[0] != p[1]}
    read = {p: jnp.sum(queries[p[0]] * keys[p[1]], -1, keepdims=True) for p in pairs}
    return written, read


def solve(solved, flat, gram, values, decays, betas, zs, gain):
    rows = values[0].shape[0]
    key_key, query_key = gram
    writes = []
    carried = [decays[0]]
    for t in range(1, STEPS):
        carried.append(carried[-1] * decays[t])
    spread = jnp.concatenate([gain, gain], axis=1)
    for t in range(STEPS):
        read = solved[0:rows, t, :] * carried[t]
        out = solved[0:rows, 4 + t, :] * carried[t]
        writes = [w * decays[t] for w in writes]
        for s in range(t):
            read = read + writes[s] * key_key[t, s]
            out = out + writes[s] * query_key[t, s]
        writes.append((values[t] - read) * betas[t])
        out = out + writes[t] * query_key[t, t]
        square = out * out
        norm = jnp.concatenate(
            [
                jnp.broadcast_to(
                    lax.rsqrt(
                        jnp.mean(square[:, h * HEAD : (h + 1) * HEAD], -1, keepdims=True) + 1e-06
                    ),
                    (rows, HEAD),
                )
                for h in range(2)
            ],
            axis=1,
        )
        result = out * norm * spread * (zs[t] * jax.nn.sigmoid(zs[t]))
        for h in range(2):
            flat[h, pl.ds(t, rows, stride=STEPS), :] = result[:, h * HEAD : (h + 1) * HEAD]
    return writes, carried[-1]


def write_side(left, right, keys, writes, carried):
    rows = keys[0].shape[0]
    left[12:16] = jnp.zeros_like(left[12:16])
    for t in range(STEPS):
        high, low = split16(keys[t])
        left[t, 0:rows, :] = high
        left[4 + t, 0:rows, :] = high
        left[8 + t, 0:rows, :] = low
        high, low = split16(writes[t])
        right[t, 0:rows, :] = high
        right[4 + t, 0:rows, :] = low
        right[8 + t, 0:rows, :] = high
    right[12, 0:rows, :] = carried


def updated(left, right, row, blocks):
    lhs = left[:, row, :].astype(BF16)
    rhs = right[:, row, :]
    update = lax.dot_general(
        lhs, rhs.astype(BF16), (((0,), (0,)), ((), ())), preferred_element_type=F32
    )
    for h in range(2):
        cut = slice(h * HEAD, (h + 1) * HEAD)
        yield blocks[h] * rhs[12:13, cut] + update[:, cut]


class Reduction:
    def __init__(self, place, scratch, weight):
        self.x, self.high, self.core = place
        (
            self.give, self.own, self.got, self.pass_on, self.passed, self.half, self.half_got,
            self.blocks, gs, gr, ps, pr, hs, hr, rs, rr, ms, mr,
        ) = scratch
        self.weight = weight
        self.width = self.give.shape[2]
        mate, far = self.peers()[:2]
        self.gives = [self.to(mate, self.give.at[k], self.got.at[k], gs.at[k], gr.at[k]) for k in range(4)]
        self.passes = [
            self.to(self.ring(k), self.pass_on.at[k - 1], self.passed.at[k - 1], ps.at[k - 1], pr.at[k - 1])
            for k in range(1, 4)
        ]
        self.swap = self.to(far, self.half, self.half_got, hs, hr)
        self.mine = self.x * 2 + self.core
        own = self.blocks.at[self.mine]
        self.rings = [self.to(self.ring(k), own, own, rs.at[k - 1], rr.at[k - 1]) for k in range(1, 4)]
        self.mates = []
        for k in range(4):
            block = self.blocks.at[self.at_x(k) * 2 + self.core]
            self.mates.append(self.to(mate, block, block, ms.at[k], mr.at[k]))

    def peers(self):
        here = self.x * 4 + self.high * 2
        return (
            here + 1 - self.core, self.x * 4 + (1 - self.high) * 2 + self.core,
            self.ring(2), self.ring(1), self.ring(3),
        )

    def at_x(self, k):
        return lax.rem(self.x + k, 4)

    def ring(self, k):
        return self.at_x(k) * 4 + self.high * 2 + self.core

    def to(self, peer, src, dst, send, recv):
        return pltpu.make_async_remote_copy(
            src_ref=src, dst_ref=dst, send_sem=send, recv_sem=recv,
            device_id={"tp": peer}, device_id_type=MESH,
        )

    def term(self, gated, block):
        cut = pl.ds(pl.multiple_of(block * self.width, self.width), self.width)
        return jnp.dot(gated, self.weight[:, cut], preferred_element_type=F32)

    order = (2, 1, 3, 0)

    def begin(self, gated):
        for k in self.order:
            self.give[k] = self.term(gated, self.at_x(k) * 2 + 1 - self.core).astype(BF16)
            self.gives[k].start()
        for k in self.order:
            self.own[k] = self.term(gated, self.at_x(k) * 2 + self.core)

    def along_x(self):
        for k in self.order:
            self.gives[k].wait_recv()
            total = self.own[k] + self.got[k].astype(F32)
            if k:
                self.pass_on[k - 1] = total.astype(BF16)
                self.passes[k - 1].start()
            else:
                self.own[0] = total

    def along_z(self):
        total = self.own[0]
        for k in (1, 3, 2):
            self.passes[k - 1].wait_recv()
            total = total + self.passed[k - 1].astype(F32)
        self.half[...] = total.astype(BF16)
        self.swap.start()

    def back_x(self):
        self.swap.wait_recv()
        self.blocks[self.mine] = (self.half[...].astype(F32) + self.half_got[...].astype(F32)).astype(BF16)
        for k in (2, 1, 3):
            self.rings[k - 1].start()
        self.mates[0].start()

    def back_core(self):
        for k in (1, 3, 2):
            self.rings[k - 1].wait_recv()
            self.mates[4 - k].start()

    def end(self):
        for k in range(4):
            self.mates[k].wait_recv()

    def drain(self):
        for copy in self.gives + self.passes + [self.swap] + self.rings + self.mates:
            copy.wait_send()

    @staticmethod
    def scratch(rows, width):
        dma = pltpu.SemaphoreType.DMA
        block = (rows, width)
        return [
            VMEM((4,) + block, BF16), VMEM((4,) + block, F32), VMEM((4,) + block, BF16),
            VMEM((3,) + block, BF16), VMEM((3,) + block, BF16),
            VMEM(block, BF16), VMEM(block, BF16), VMEM((8,) + block, BF16),
            dma((4,)), dma((4,)), dma((3,)), dma((3,)), dma, dma,
            dma((3,)), dma((3,)), dma((4,)), dma((4,)),
        ]


class ShortReduction:
    def __init__(self, place, scratch, weight):
        self.x, self.high, self.core = place
        (
            self.give, self.own, self.got, self.half, self.half_got, self.blocks,
            gs, gr, hs, hr, bs, br,
        ) = scratch
        self.weight = weight
        self.width = self.give.shape[2]
        self.mine = self.x * 2 + self.core
        self.gives, self.backs, self.awaited = [], [], []
        for at, (dx, dc) in enumerate(self.order):
            peer = self.device(dx, dc)
            self.gives.append(self.to(peer, self.give.at[at], self.got.at[at], gs.at[at], gr.at[at]))
            own = self.blocks.at[self.mine]
            self.backs.append(self.to(peer, own, own, bs.at[at], br.at[at]))
            theirs = self.blocks.at[self.block(-dx, dc)]
            self.awaited.append(self.to(self.device(-dx, dc), own, theirs, bs.at[at], br.at[at]))
        far = self.x * 4 + (1 - self.high) * 2 + self.core
        self.swap = self.to(far, self.half, self.half_got, hs, hr)

    order = ((2, 0), (2, 1), (1, 0), (1, 1), (3, 0), (3, 1), (0, 1))

    def toward(self, dx, dc):
        return lax.rem(self.x + dx + 4, 4), 1 - self.core if dc else self.core

    def device(self, dx, dc):
        x, core = self.toward(dx, dc)
        return x * 4 + self.high * 2 + core

    def block(self, dx, dc):
        x, core = self.toward(dx, dc)
        return x * 2 + core

    def peers(self):
        far = self.x * 4 + (1 - self.high) * 2 + self.core
        return [far] + [self.device(dx, dc) for dx, dc in self.order]

    to = Reduction.to
    term = Reduction.term

    def begin(self, gated):
        for at, (dx, dc) in enumerate(self.order):
            self.give[at] = self.term(gated, self.block(dx, dc)).astype(BF16)
            self.gives[at].start()
        self.own[...] = self.term(gated, self.mine)

    def along_z(self):
        total = self.own[...]
        for at in (6, 2, 3, 4, 5, 0, 1):
            self.gives[at].wait_recv()
            total = total + self.got[at].astype(F32)
        self.half[...] = total.astype(BF16)
        self.swap.start()

    def back(self):
        self.swap.wait_recv()
        self.blocks[self.mine] = (self.half[...].astype(F32) + self.half_got[...].astype(F32)).astype(BF16)
        for copy in self.backs:
            copy.start()

    def end(self):
        for copy in self.awaited:
            copy.wait_recv()

    def drain(self):
        for copy in self.gives + [self.swap] + self.backs:
            copy.wait_send()

    @staticmethod
    def scratch(rows, width):
        dma = pltpu.SemaphoreType.DMA
        block = (rows, width)
        return [
            VMEM((7,) + block, BF16), VMEM(block, F32), VMEM((7,) + block, BF16),
            VMEM(block, BF16), VMEM(block, BF16), VMEM((8,) + block, BF16),
            dma((7,)), dma((7,)), dma, dma, dma((7,)), dma((7,)),
        ]


REDUCTION = 18


def decode_kernel(
    crossing, slots, partner, decay_log, time_bias,
    state_in, conv_in, mixed_in, gates_in, zgate_in, weight_in, gain_in, out_weight_in,
    states_out, hidden_all, hidden_moved,
    states, moved, store_sems, conv, mixed, gates, zgate, weight, gain, out_weight, load_sems,
    fresh, gate_rows, left, right, solved, flat, left_m, right_m, solved_m, flat_m,
    rows_out, conv_rows, conv_out, held_0, held_1, held_2, conv_held, turned, conv_turned, landed, conv_landed,
    send1, recv1, csend1, crecv1, send2, recv2, csend2, crecv2,
    *reductions,
):
    rows = mixed.shape[0]
    tp = lax.axis_index("tp")
    me = lax.axis_index("req")
    core = lax.rem(tp, 2)
    place = (tp // 4, lax.rem(tp // 2, 2), core)
    half, mine = lax.rem(me // 4, 2), number_of(me)
    order = ordered(partner)
    slot = [slots[0, order[j]] for j in range(MOVE)]
    streams = list(range(crossing, MOVE)) + list(range(crossing))

    def first_half(j):
        return 1 - half if j < crossing else half
    held = (held_0, held_1, held_2)

    loads = [
        pltpu.make_async_copy(src, dst, load_sems.at[at])
        for at, (src, dst) in enumerate(
            (
                (conv_in, conv), (state_in, states), (mixed_in, mixed),
                (gates_in, gates), (weight_in, weight), (zgate_in, zgate), (gain_in, gain),
                (out_weight_in, out_weight),
            )
        )
    ]
    for load in loads:
        load.start()

    everyone = Reduction(place, reductions[:REDUCTION], out_weight)
    movers = ShortReduction(place, reductions[REDUCTION:], out_weight)
    barrier = pltpu.get_barrier_semaphore()

    def greet(k, carry):
        peer = member(lax.rem(half + 1 + k // PIECES, 2), lax.rem(mine + k, PIECES))

        @pl.when(peer != me)
        def _():
            pl.semaphore_signal(barrier, inc=1, device_id={"req": peer}, device_id_type=MESH)

        return carry

    tp_peers = movers.peers()
    for peer in tp_peers:
        pl.semaphore_signal(barrier, inc=1, device_id={"tp": peer}, device_id_type=MESH)
    lax.fori_loop(0 if crossing else PIECES, GROUPS, greet, 0)

    loads[0].wait()
    conv_rows[...] = jnp.zeros_like(conv_rows)
    for j in range(MOVE):
        for tap in range(3):
            for part in range(4):
                conv_rows[j, pl.ds(tap * 4 + part, 1), :] = conv[
                    slot[j], tap, :, part * LANES : (part + 1) * LANES
                ]
        conv_out[j] = conv_rows[j].astype(BF16)
    loads[1].wait()

    def pack(piece, carry):
        start = pl.multiple_of(lax.rem(piece, 8) * TILE, TILE)
        for j in range(MOVE):
            rows_out[j, piece] = states[slot[j], piece // 8, pl.ds(start, TILE), :].astype(BF16)
        return carry

    lax.fori_loop(0, PIECES, pack, 0)

    for load in loads[2:7]:
        load.wait()
    fresh[...] = mixed[...].astype(F32)
    latest = [fresh[:, t, :] for t in range(STEPS)]
    gate_rows[...] = jnp.zeros_like(gate_rows)
    for t in range(STEPS):
        for kind in range(2):
            at = t * 4 + kind * 2
            gate_rows[at : at + 2, 0:rows] = gates[t, kind]
    columns = gate_rows[...].T

    def both(at):
        return jnp.concatenate(
            [
                jnp.broadcast_to(columns[0:rows, at + h : at + h + 1], (rows, HEAD))
                for h in range(2)
            ],
            axis=1,
        )

    rate = jnp.exp(halves(decay_log[0], decay_log[1], (1, 2 * HEAD)))
    bias = halves(time_bias[0], time_bias[1], (1, 2 * HEAD))
    decays, betas, zs = [], [], []
    for t in range(STEPS):
        a = both(t * 4) + bias
        soft = jnp.maximum(a, 0.0) + jnp.log1p(jnp.exp(-jnp.abs(a)))
        decays.append(jnp.exp(-rate * soft))
        betas.append(jax.nn.sigmoid(both(t * 4 + 2)))
        zs.append(zgate[:, t, :].astype(F32))
    spread = gain[...]

    left[...] = jnp.zeros_like(left)
    right[...] = jnp.zeros_like(right)
    window = [conv[:, tap, 0, :] for tap in range(3)] + latest
    queries, keys, values = convolved(window, weight)
    read_side(left, queries, keys)
    for r in range(rows):
        lhs = left[:, r, :].astype(BF16)
        for h in range(2):
            block = states[r, h]
            high = block.astype(BF16)
            low = (block - high.astype(F32)).astype(BF16)
            product = jnp.dot(lhs, high, preferred_element_type=F32) + jnp.dot(
                lhs, low, preferred_element_type=F32
            )
            solved[r, :, h * HEAD : (h + 1) * HEAD] = product[0:8] + product[8:16]
    gram = products(queries, keys)
    writes, carried = solve(solved, flat, gram, values, decays, betas, zs, spread)
    write_side(left, right, keys, writes, carried)

    def picked(value):
        at_row = lax.broadcasted_iota(jnp.int32, value.shape, 0)
        target = (8, value.shape[1])
        at_out = lax.broadcasted_iota(jnp.int32, target, 0)
        result = jnp.zeros(target, F32)
        for j in range(MOVE):
            row = jnp.sum(jnp.where(at_row == slot[j], value, 0.0), axis=0, keepdims=True)
            result = jnp.where(at_out == j, jnp.broadcast_to(row, target), result)
        return result

    latest_m = [picked(value) for value in latest]
    decays_m = [picked(value) for value in decays]
    betas_m = [picked(value) for value in betas]
    zs_m = [picked(value) for value in zs]

    pl.semaphore_wait(barrier, (GROUPS if crossing else PIECES) - 1 + len(tp_peers))

    def first(j, piece, peer):
        return pltpu.make_async_remote_copy(
            src_ref=rows_out.at[j, piece], dst_ref=held[j].at[mine], send_sem=send1.at[j, piece],
            recv_sem=recv1.at[j, mine], device_id={"req": peer}, device_id_type=MESH,
        )

    def conv_first(j, peer):
        return pltpu.make_async_remote_copy(
            src_ref=conv_out.at[j], dst_ref=conv_held.at[mine], send_sem=csend1.at[j],
            recv_sem=crecv1.at[mine], device_id={"req": peer}, device_id_type=MESH,
        )

    for j in range(MOVE):
        peer = member(first_half(j), CONV_PIECE[j])

        @pl.when(peer != me)
        def _():
            conv_first(j, peer).start()

        @pl.when(peer == me)
        def _():
            conv_held[mine] = conv_out[j]

    for j in range(MOVE):

        def send_piece(k, carry):
            piece = lax.rem(mine + k, PIECES)
            peer = member(first_half(j), piece)

            @pl.when(peer != me)
            def _():
                first(j, piece, peer).start()

            @pl.when(peer == me)
            def _():
                held[j][mine] = rows_out[j, piece]

            return carry

        lax.fori_loop(0, PIECES, send_piece, 0)

    loads[7].wait()
    everyone.begin(jnp.concatenate([flat[0], flat[1]], axis=1).astype(BF16))
    for r in range(rows):
        new = list(updated(left, right, r, [states[r, h] for h in range(2)]))
        for h in range(2):
            states[r, h] = new[h]
    stores = [
        pltpu.make_async_copy(src, dst, store_sems.at[at])
        for at, (src, dst) in enumerate(
            (
                (states, states_out.at[pl.ds(0, rows)]), (everyone.blocks, hidden_all),
                (moved, states_out.at[pl.ds(rows, MOVE)]),
                (movers.blocks, hidden_moved),
            )
        )
    ]
    stores[0].start()
    everyone.along_x()

    def second(j, number):
        return pltpu.make_async_remote_copy(
            src_ref=turned.at[j, number], dst_ref=landed.at[j, mine], send_sem=send2.at[j, number],
            recv_sem=recv2.at[j, mine], device_id={"req": member(half, number)}, device_id_type=MESH,
        )

    def conv_second(j, number):
        return pltpu.make_async_remote_copy(
            src_ref=conv_turned.at[number], dst_ref=conv_landed.at[j], send_sem=csend2.at[number],
            recv_sem=crecv2.at[j], device_id={"req": member(half, number)}, device_id_type=MESH,
        )

    for j in streams:

        def wait_first(k, carry):
            number = lax.rem(mine + k, PIECES)
            source = member(first_half(j), number)

            @pl.when(source != me)
            def _():
                pltpu.make_async_remote_copy(
                    src_ref=rows_out.at[j, 0], dst_ref=held[j].at[number], send_sem=send1.at[j, 0],
                    recv_sem=recv1.at[j, number], device_id={"req": source}, device_id_type=MESH,
                ).wait_recv()

            return carry

        lax.fori_loop(0, PIECES, wait_first, 0)

        def turn(k, carry):
            number = lax.rem(mine + k, PIECES)
            source = partner[order[j], member(half, number)]
            turned[j, number] = held[j][number_of(source)]

            @pl.when(k > 0)
            def _():
                second(j, number).start()

            return carry

        lax.fori_loop(0, PIECES, turn, 0)
        landed[j, mine] = turned[j, mine]

        @pl.when(mine == CONV_PIECE[j])
        def _():
            def wait_conv(k, carry):
                number = lax.rem(mine + k, PIECES)
                source = member(first_half(j), number)

                @pl.when(source != me)
                def _():
                    pltpu.make_async_remote_copy(
                        src_ref=conv_out.at[0], dst_ref=conv_held.at[number], send_sem=csend1.at[0],
                        recv_sem=crecv1.at[number], device_id={"req": source}, device_id_type=MESH,
                    ).wait_recv()

                return carry

            lax.fori_loop(0, PIECES, wait_conv, 0)

            def turn_conv(k, carry):
                number = lax.rem(mine + k, PIECES)
                source = partner[order[j], member(half, number)]
                conv_turned[number] = conv_held[number_of(source)]

                @pl.when(k > 0)
                def _():
                    conv_second(j, number).start()

                return carry

            lax.fori_loop(0, PIECES, turn_conv, 0)
            conv_landed[j] = conv_turned[mine]

    everyone.along_z()

    for j in range(MOVE):
        @pl.when(mine != CONV_PIECE[j])
        def _():
            conv_second(j, CONV_PIECE[j]).wait_recv()

    at_out = lax.broadcasted_iota(jnp.int32, (8, LANES), 0)
    window_m = []
    for tap in range(3):
        parts = []
        for part in range(4):
            at = tap * 4 + part
            value = jnp.zeros((8, LANES), F32)
            for j in range(MOVE):
                row = conv_landed[j].astype(F32)[at : at + 1, :]
                value = jnp.where(at_out == j, jnp.broadcast_to(row, (8, LANES)), value)
            parts.append(value)
        window_m.append(jnp.concatenate(parts, axis=1))
    left_m[...] = jnp.zeros_like(left_m)
    right_m[...] = jnp.zeros_like(right_m)
    solved_m[...] = jnp.zeros_like(solved_m)
    queries, keys, values = convolved(window_m + latest_m, weight)
    read_side(left_m, queries, keys)
    gram = products(queries, keys)

    for j in streams:

        def wait_second(k, carry):
            piece = lax.rem(mine + k, PIECES)
            pltpu.make_async_remote_copy(
                src_ref=turned.at[j, 0], dst_ref=landed.at[j, piece], send_sem=send2.at[j, 0],
                recv_sem=recv2.at[j, piece], device_id={"req": member(half, piece)},
                device_id_type=MESH,
            ).wait_recv()
            return carry

        lax.fori_loop(1, PIECES, wait_second, 0)
        lhs = left_m[:, j, :].astype(BF16)
        for h in range(2):
            block = landed[j, h * 8 : (h + 1) * 8].reshape(HEAD, HEAD)
            product = jnp.dot(lhs, block, preferred_element_type=F32)
            solved_m[j, :, h * HEAD : (h + 1) * HEAD] = product[0:8] + product[8:16]

    writes, carried = solve(
        solved_m, flat_m, gram, values, decays_m, betas_m, zs_m, spread
    )
    movers.begin(jnp.concatenate([flat_m[0, 0:16], flat_m[1, 0:16]], axis=1).astype(BF16))
    write_side(left_m, right_m, keys, writes, carried)
    movers.along_z()
    everyone.back_x()
    for j in range(MOVE):
        blocks = [
            landed[j, h * 8 : (h + 1) * 8].reshape(HEAD, HEAD).astype(F32) for h in range(2)
        ]
        for h, new in enumerate(updated(left_m, right_m, j, blocks)):
            moved[j, h] = new
    stores[2].start()
    everyone.back_core()

    for j in range(MOVE):

        def done_first(piece, carry):
            peer = member(first_half(j), piece)

            @pl.when(peer != me)
            def _():
                first(j, piece, peer).wait_send()

            return carry

        lax.fori_loop(0, PIECES, done_first, 0)
        peer = member(first_half(j), CONV_PIECE[j])

        @pl.when(peer != me)
        def _():
            conv_first(j, peer).wait_send()

        def done_second(k, carry):
            second(j, lax.rem(mine + k, PIECES)).wait_send()
            return carry

        lax.fori_loop(1, PIECES, done_second, 0)

        @pl.when(mine == CONV_PIECE[j])
        def _():
            def done_conv(k, carry):
                conv_second(j, lax.rem(mine + k, PIECES)).wait_send()
                return carry

            lax.fori_loop(1, PIECES, done_conv, 0)

    everyone.end()
    stores[1].start()
    everyone.drain()
    movers.back()
    movers.end()
    stores[3].start()
    movers.drain()
    for store in stores:
        store.wait()


def decode(
    crossing, slots, partner, decay_log, time_bias, state, conv, mixed, gates, zgate, weight, gain, out_weight
):
    rows = state.shape[0]
    width = out_weight.shape[1] // 8
    tile = (TILE, LANES)
    dma = pltpu.SemaphoreType.DMA
    smem = pl.BlockSpec(memory_space=pltpu.SMEM)
    anywhere = pl.BlockSpec(memory_space=pl.ANY)
    arrays = (state, conv, mixed, gates, zgate, weight, gain, out_weight)

    def working(count, padded):
        return [
            VMEM((16, padded, HEAD), F32),
            VMEM((16, padded, 2 * HEAD), F32),
            VMEM((count, 8, 2 * HEAD), F32),
            VMEM((2, count * STEPS, HEAD), F32),
        ]

    return pl.pallas_call(
        functools.partial(decode_kernel, crossing),
        out_shape=(
            jax.ShapeDtypeStruct((rows + MOVE,) + state.shape[1:], F32),
            jax.ShapeDtypeStruct((8, rows * STEPS, width), BF16),
            jax.ShapeDtypeStruct((8, TILE, width), BF16),
        ),
        in_specs=[smem] * 4 + [anywhere] * len(arrays),
        out_specs=(anywhere,) * 3,
        scratch_shapes=[VMEM(state.shape, F32), VMEM((MOVE,) + state.shape[1:], F32), dma((4,))]
        + [VMEM(a.shape, a.dtype) for a in arrays[1:]]
        + [dma((len(arrays),)), VMEM(mixed.shape, F32), VMEM((LANES, LANES), F32)]
        + working(rows, 16)
        + working(8, 8)
        + [
            VMEM((MOVE, PIECES) + tile, BF16),
            VMEM((MOVE,) + tile, F32),
            VMEM((MOVE,) + tile, BF16),
            VMEM((PIECES,) + tile, BF16),
            VMEM((PIECES,) + tile, BF16),
            VMEM((PIECES,) + tile, BF16),
            VMEM((PIECES,) + tile, BF16),
            VMEM((MOVE, PIECES) + tile, BF16),
            VMEM((PIECES,) + tile, BF16),
            VMEM((MOVE, PIECES) + tile, BF16),
            VMEM((MOVE,) + tile, BF16),
            dma((MOVE, PIECES)), dma((MOVE, PIECES)), dma((MOVE,)), dma((PIECES,)),
            dma((MOVE, PIECES)), dma((MOVE, PIECES)), dma((PIECES,)), dma((MOVE,)),
        ]
        + Reduction.scratch(rows * STEPS, width)
        + ShortReduction.scratch(TILE, width),
        compiler_params=pltpu.CompilerParams(
            collective_id=crossing, has_side_effects=True, vmem_limit_bytes=58 << 20
        ),
        name="decode",
    )(slots, partner, decay_log, time_bias, *arrays)


def place_kernel(
    slots, partner, states, hidden_all, hidden_moved, mixed, hidden, new_state, new_conv,
    held, kept, changed, latest, fresh, out, load_sems, store_sems,
):
    rows = mixed.shape[0]
    width = hidden_all.shape[2]
    slot = [slots[0, at] for at in ordered(partner)]
    loads, stores = [], []
    for r in range(rows):
        source = r
        for j in range(MOVE):
            source = jnp.where(slot[j] == r, rows + j, source)
        loads.append(pltpu.make_async_copy(states.at[source], held.at[r], load_sems.at[r]))
        stores.append(pltpu.make_async_copy(held.at[r], new_state.at[r], store_sems.at[r]))
    for at, (src, dst) in enumerate(((hidden_all, kept), (hidden_moved, changed), (mixed, latest))):
        loads.append(pltpu.make_async_copy(src, dst, load_sems.at[rows + at]))
    stores.append(pltpu.make_async_copy(fresh, new_conv, store_sems.at[rows]))
    for block in range(8):
        cut = pl.ds(block * width, width)
        stores.append(
            pltpu.make_async_copy(
                out.at[:, :, cut], hidden.at[:, :, cut], store_sems.at[rows + 1 + block]
            )
        )
    for load in loads[rows:] + loads[:rows]:
        load.start()
    for load in loads[rows:]:
        load.wait()
    values = latest[...].astype(F32)
    for tap in range(3):
        fresh[:, tap, 0, :] = values[:, tap + 1, :]
    stores[rows].start()
    for block in range(8):
        cut = slice(block * width, (block + 1) * width)
        stay = kept[block].astype(F32)
        came = changed[block].astype(F32)
        for r in range(rows):
            value = stay[r * STEPS : (r + 1) * STEPS, :]
            for j in range(MOVE):
                value = jnp.where(slot[j] == r, came[j * STEPS : (j + 1) * STEPS, :], value)
            out[r, :, cut] = value.astype(BF16)
        stores[rows + 1 + block].start()
        for r in range(rows * block // 8, rows * (block + 1) // 8):
            loads[r].wait()
            stores[r].start()
    for store in stores:
        store.wait()


def place(slots, partner, states, hidden_all, hidden_moved, mixed):
    rows = mixed.shape[0]
    dma = pltpu.SemaphoreType.DMA
    anywhere = pl.BlockSpec(memory_space=pl.ANY)
    hidden = (rows, STEPS, 8 * hidden_all.shape[2])
    conv = (rows, TAPS - 1, 1, mixed.shape[2])
    return pl.pallas_call(
        place_kernel,
        out_shape=(
            jax.ShapeDtypeStruct(hidden, BF16),
            jax.ShapeDtypeStruct((rows,) + states.shape[1:], F32),
            jax.ShapeDtypeStruct(conv, F32),
        ),
        in_specs=[pl.BlockSpec(memory_space=pltpu.SMEM)] * 2 + [anywhere] * 4,
        out_specs=(anywhere,) * 3,
        scratch_shapes=[
            VMEM((rows,) + states.shape[1:], F32), VMEM(hidden_all.shape, BF16),
            VMEM(hidden_moved.shape, BF16), VMEM(mixed.shape, BF16), VMEM(conv, F32),
            VMEM(hidden, BF16), dma((rows + 3,)), dma((rows + 9,)),
        ],
        compiler_params=pltpu.CompilerParams(vmem_limit_bytes=58 << 20),
        name="place",
    )(slots, partner, states, hidden_all, hidden_moved, mixed)


def per_device(
    state,
    conv_state,
    mixed,
    gates,
    output_gate,
    conv_weight,
    decay_log,
    time_bias,
    norm_gain,
    out_weight,
    partner,
    moved_slots,
):
    fresh = mixed.reshape(mixed.shape[0], mixed.shape[1], mixed.shape[3])
    masks = partner.T
    states, hidden_all, hidden_moved = lax.switch(
        jnp.sum(lax.rem(partner[0] // 4, 2)),
        [functools.partial(decode, crossing) for crossing in range(MOVE + 1)],
        moved_slots, masks, decay_log, time_bias, state, conv_state.transpose(0, 2, 1, 3),
        fresh, gates.transpose(1, 2, 3, 0), output_gate, conv_weight, norm_gain.reshape(1, -1),
        out_weight,
    )
    hidden, new_state, new_conv = place(
        moved_slots, masks, states, hidden_all, hidden_moved, fresh
    )
    return (hidden, new_state, new_conv.transpose(0, 2, 1, 3))


def solution(mesh):
    placed = (
        P("req", "tp", None, None),
        P("req", "tp", None, None),
        P("req", None, "tp", None),
        P("req", None, None, "tp"),
        P("req", None, "tp"),
        P("tp", None, None),
        P("tp"),
        P("tp"),
        P(),
        P("tp", None),
        P(),
        P("req", None),
    )
    return jax.shard_map(
        per_device,
        mesh=mesh,
        in_specs=placed,
        out_specs=(P("req", None, None), P("req", "tp", None, None), P("req", "tp", None, None)),
        check_vma=False,
    )
```

```python
import functools

import jax
import jax.numpy as jnp
from jax import lax
from jax.experimental import pallas as pl
from jax.experimental.pallas import tpu as pltpu
from jax.sharding import PartitionSpec as P

MESH = pl.DeviceIdType.MESH
F32 = jnp.float32
BF16 = jnp.bfloat16
VMEM = pltpu.VMEM
GROUPS, MOVE, PIECES, TILE, LANES = 32, 3, 16, 16, 128
CONV_PIECE = (2, 7, 12)
HEAD, TAPS, STEPS = 128, 4, 4


def member(half, number):
    return number // 4 * 8 + half * 4 + lax.rem(number, 4)


def number_of(group):
    return group // 8 * 4 + lax.rem(group, 4)


def ordered(partner):
    crossing = [lax.rem(partner[j, 0] // 4, 2) for j in range(MOVE)]
    count = crossing[0] + crossing[1] + crossing[2]
    before = [0, crossing[0], crossing[0] + crossing[1]]
    places = [
        jnp.where(crossing[j] == 1, before[j], count + j - before[j]) for j in range(MOVE)
    ]
    return [
        sum(jnp.where(places[j] == at, j, 0) for j in range(MOVE)) for at in range(MOVE)
    ]


def split16(value):
    high = value.astype(BF16)
    return high.astype(F32), value - high.astype(F32)


def halves(scalar_a, scalar_b, shape):
    lane = lax.broadcasted_iota(jnp.int32, shape, len(shape) - 1)
    return jnp.where(lane < HEAD, scalar_a, scalar_b)


def convolved(window, weight):
    queries, keys, values = [], [], []
    for t in range(STEPS):
        total = window[t] * weight[0, 0:1, :]
        for tap in range(1, TAPS):
            total = total + window[t + tap] * weight[0, tap : tap + 1, :]
        c = total * jax.nn.sigmoid(total)
        q, k = c[:, :HEAD], c[:, HEAD : 2 * HEAD]
        queries.append(
            q * lax.rsqrt(jnp.sum(q * q, -1, keepdims=True) + 1e-06) / jnp.sqrt(jnp.float32(HEAD))
        )
        keys.append(k * lax.rsqrt(jnp.sum(k * k, -1, keepdims=True) + 1e-06))
        values.append(c[:, 2 * HEAD :])
    return queries, keys, values


def read_side(left, queries, keys):
    rows = keys[0].shape[0]
    for t in range(STEPS):
        for at, part in enumerate(split16(keys[t]) + split16(queries[t])):
            left[t + (0, 8, 4, 12)[at], 0:rows, :] = part


def products(queries, keys):
    pairs = [(t, s) for t in range(STEPS) for s in range(t + 1)]
    written = {p: jnp.sum(keys[p[0]] * keys[p[1]], -1, keepdims=True) for p in pairs if p[0] != p[1]}
    read = {p: jnp.sum(queries[p[0]] * keys[p[1]], -1, keepdims=True) for p in pairs}
    return written, read


def solve(solved, flat, gram, values, decays, betas, zs, gain):
    rows = values[0].shape[0]
    key_key, query_key = gram
    writes = []
    carried = [decays[0]]
    for t in range(1, STEPS):
        carried.append(carried[-1] * decays[t])
    spread = jnp.concatenate([gain, gain], axis=1)
    for t in range(STEPS):
        read = solved[0:rows, t, :] * carried[t]
        out = solved[0:rows, 4 + t, :] * carried[t]
        writes = [w * decays[t] for w in writes]
        for s in range(t):
            read = read + writes[s] * key_key[t, s]
            out = out + writes[s] * query_key[t, s]
        writes.append((values[t] - read) * betas[t])
        out = out + writes[t] * query_key[t, t]
        square = out * out
        norm = jnp.concatenate(
            [
                jnp.broadcast_to(
                    lax.rsqrt(
                        jnp.mean(square[:, h * HEAD : (h + 1) * HEAD], -1, keepdims=True) + 1e-06
                    ),
                    (rows, HEAD),
                )
                for h in range(2)
            ],
            axis=1,
        )
        result = out * norm * spread * (zs[t] * jax.nn.sigmoid(zs[t]))
        for h in range(2):
            flat[h, pl.ds(t, rows, stride=STEPS), :] = result[:, h * HEAD : (h + 1) * HEAD]
    return writes, carried[-1]


def write_side(left, right, keys, writes, carried):
    rows = keys[0].shape[0]
    left[12:16] = jnp.zeros_like(left[12:16])
    for t in range(STEPS):
        high, low = split16(keys[t])
        left[t, 0:rows, :] = high
        left[4 + t, 0:rows, :] = high
        left[8 + t, 0:rows, :] = low
        high, low = split16(writes[t])
        right[t, 0:rows, :] = high
        right[4 + t, 0:rows, :] = low
        right[8 + t, 0:rows, :] = high
    right[12, 0:rows, :] = carried


def updated(left, right, row, blocks):
    lhs = left[:, row, :].astype(BF16)
    rhs = right[:, row, :]
    update = lax.dot_general(
        lhs, rhs.astype(BF16), (((0,), (0,)), ((), ())), preferred_element_type=F32
    )
    for h in range(2):
        cut = slice(h * HEAD, (h + 1) * HEAD)
        yield blocks[h] * rhs[12:13, cut] + update[:, cut]


class Reduction:
    def __init__(self, place, scratch, weight):
        self.x, self.high, self.core = place
        (
            self.give, self.own, self.got, self.pass_on, self.passed, self.half, self.half_got,
            self.blocks, gs, gr, ps, pr, hs, hr, rs, rr, ms, mr,
        ) = scratch
        self.weight = weight
        self.width = self.give.shape[2]
        mate, far = self.peers()[:2]
        self.gives = [self.to(mate, self.give.at[k], self.got.at[k], gs.at[k], gr.at[k]) for k in range(4)]
        self.passes = [
            self.to(self.ring(k), self.pass_on.at[k - 1], self.passed.at[k - 1], ps.at[k - 1], pr.at[k - 1])
            for k in range(1, 4)
        ]
        self.swap = self.to(far, self.half, self.half_got, hs, hr)
        self.mine = self.x * 2 + self.core
        own = self.blocks.at[self.mine]
        self.rings = [self.to(self.ring(k), own, own, rs.at[k - 1], rr.at[k - 1]) for k in range(1, 4)]
        self.mates = []
        for k in range(4):
            block = self.blocks.at[self.at_x(k) * 2 + self.core]
            self.mates.append(self.to(mate, block, block, ms.at[k], mr.at[k]))

    def peers(self):
        here = self.x * 4 + self.high * 2
        return (
            here + 1 - self.core, self.x * 4 + (1 - self.high) * 2 + self.core,
            self.ring(2), self.ring(1), self.ring(3),
        )

    def at_x(self, k):
        return lax.rem(self.x + k, 4)

    def ring(self, k):
        return self.at_x(k) * 4 + self.high * 2 + self.core

    def to(self, peer, src, dst, send, recv):
        return pltpu.make_async_remote_copy(
            src_ref=src, dst_ref=dst, send_sem=send, recv_sem=recv,
            device_id={"tp": peer}, device_id_type=MESH,
        )

    def term(self, gated, block):
        cut = pl.ds(pl.multiple_of(block * self.width, self.width), self.width)
        return jnp.dot(gated, self.weight[:, cut], preferred_element_type=F32)

    order = (2, 1, 3, 0)

    def begin(self, gated):
        for k in self.order:
            self.give[k] = self.term(gated, self.at_x(k) * 2 + 1 - self.core).astype(BF16)
            self.gives[k].start()
        for k in self.order:
            self.own[k] = self.term(gated, self.at_x(k) * 2 + self.core)

    def along_x(self):
        for k in self.order:
            self.gives[k].wait_recv()
            total = self.own[k] + self.got[k].astype(F32)
            if k:
                self.pass_on[k - 1] = total.astype(BF16)
                self.passes[k - 1].start()
            else:
                self.own[0] = total

    def along_z(self):
        total = self.own[0]
        for k in (1, 3, 2):
            self.passes[k - 1].wait_recv()
            total = total + self.passed[k - 1].astype(F32)
        self.half[...] = total.astype(BF16)
        self.swap.start()

    def back_x(self):
        self.swap.wait_recv()
        self.blocks[self.mine] = (self.half[...].astype(F32) + self.half_got[...].astype(F32)).astype(BF16)
        for k in (2, 1, 3):
            self.rings[k - 1].start()
        self.mates[0].start()

    def back_core(self):
        for k in (1, 3, 2):
            self.rings[k - 1].wait_recv()
            self.mates[4 - k].start()

    def end(self):
        for k in range(4):
            self.mates[k].wait_recv()

    def drain(self):
        for copy in self.gives + self.passes + [self.swap] + self.rings + self.mates:
            copy.wait_send()

    @staticmethod
    def scratch(rows, width):
        dma = pltpu.SemaphoreType.DMA
        block = (rows, width)
        return [
            VMEM((4,) + block, BF16), VMEM((4,) + block, F32), VMEM((4,) + block, BF16),
            VMEM((3,) + block, BF16), VMEM((3,) + block, BF16),
            VMEM(block, BF16), VMEM(block, BF16), VMEM((8,) + block, BF16),
            dma((4,)), dma((4,)), dma((3,)), dma((3,)), dma, dma,
            dma((3,)), dma((3,)), dma((4,)), dma((4,)),
        ]


class ShortReduction:
    def __init__(self, place, scratch, weight):
        self.x, self.high, self.core = place
        (
            self.give, self.own, self.got, self.half, self.half_got, self.blocks,
            gs, gr, hs, hr, bs, br,
        ) = scratch
        self.weight = weight
        self.width = self.give.shape[2]
        self.mine = self.x * 2 + self.core
        self.gives, self.backs, self.awaited = [], [], []
        for at, (dx, dc) in enumerate(self.order):
            peer = self.device(dx, dc)
            self.gives.append(self.to(peer, self.give.at[at], self.got.at[at], gs.at[at], gr.at[at]))
            own = self.blocks.at[self.mine]
            self.backs.append(self.to(peer, own, own, bs.at[at], br.at[at]))
            theirs = self.blocks.at[self.block(-dx, dc)]
            self.awaited.append(self.to(self.device(-dx, dc), own, theirs, bs.at[at], br.at[at]))
        far = self.x * 4 + (1 - self.high) * 2 + self.core
        self.swap = self.to(far, self.half, self.half_got, hs, hr)

    order = ((2, 0), (2, 1), (1, 0), (1, 1), (3, 0), (3, 1), (0, 1))

    def toward(self, dx, dc):
        return lax.rem(self.x + dx + 4, 4), 1 - self.core if dc else self.core

    def device(self, dx, dc):
        x, core = self.toward(dx, dc)
        return x * 4 + self.high * 2 + core

    def block(self, dx, dc):
        x, core = self.toward(dx, dc)
        return x * 2 + core

    def peers(self):
        far = self.x * 4 + (1 - self.high) * 2 + self.core
        return [far] + [self.device(dx, dc) for dx, dc in self.order]

    to = Reduction.to
    term = Reduction.term

    def begin(self, gated):
        for at, (dx, dc) in enumerate(self.order):
            self.give[at] = self.term(gated, self.block(dx, dc)).astype(BF16)
            self.gives[at].start()
        self.own[...] = self.term(gated, self.mine)

    def along_z(self):
        total = self.own[...]
        for at in (6, 2, 3, 4, 5, 0, 1):
            self.gives[at].wait_recv()
            total = total + self.got[at].astype(F32)
        self.half[...] = total.astype(BF16)
        self.swap.start()

    def back(self):
        self.swap.wait_recv()
        self.blocks[self.mine] = (self.half[...].astype(F32) + self.half_got[...].astype(F32)).astype(BF16)
        for copy in self.backs:
            copy.start()

    def end(self):
        for copy in self.awaited:
            copy.wait_recv()

    def drain(self):
        for copy in self.gives + [self.swap] + self.backs:
            copy.wait_send()

    @staticmethod
    def scratch(rows, width):
        dma = pltpu.SemaphoreType.DMA
        block = (rows, width)
        return [
            VMEM((7,) + block, BF16), VMEM(block, F32), VMEM((7,) + block, BF16),
            VMEM(block, BF16), VMEM(block, BF16), VMEM((8,) + block, BF16),
            dma((7,)), dma((7,)), dma, dma, dma((7,)), dma((7,)),
        ]


REDUCTION = 18


def decode_kernel(
    crossing, slots, partner, decay_log, time_bias,
    state_in, conv_in, mixed_in, gates_in, zgate_in, weight_in, gain_in, out_weight_in,
    states_out, hidden_all, hidden_moved,
    states, moved, store_sems, conv, mixed, gates, zgate, weight, gain, out_weight, load_sems,
    fresh, gate_rows, left, right, solved, flat, left_m, right_m, solved_m, flat_m,
    rows_out, conv_rows, conv_out, held_0, held_1, held_2, conv_held, turned, conv_turned, landed, conv_landed,
    send1, recv1, csend1, crecv1, send2, recv2, csend2, crecv2,
    *reductions,
):
    rows = mixed.shape[0]
    tp = lax.axis_index("tp")
    me = lax.axis_index("req")
    core = lax.rem(tp, 2)
    place = (tp // 4, lax.rem(tp // 2, 2), core)
    half, mine = lax.rem(me // 4, 2), number_of(me)
    order = ordered(partner)
    slot = [slots[0, order[j]] for j in range(MOVE)]
    streams = list(range(crossing, MOVE)) + list(range(crossing))

    def first_half(j):
        return 1 - half if j < crossing else half
    held = (held_0, held_1, held_2)

    loads = [
        pltpu.make_async_copy(src, dst, load_sems.at[at])
        for at, (src, dst) in enumerate(
            (
                (conv_in, conv), (state_in, states), (mixed_in, mixed),
                (gates_in, gates), (weight_in, weight), (zgate_in, zgate), (gain_in, gain),
                (out_weight_in, out_weight),
            )
        )
    ]
    for load in loads:
        load.start()

    everyone = Reduction(place, reductions[:REDUCTION], out_weight)
    movers = ShortReduction(place, reductions[REDUCTION:], out_weight)
    barrier = pltpu.get_barrier_semaphore()

    def greet(k, carry):
        peer = member(lax.rem(half + 1 + k // PIECES, 2), lax.rem(mine + k, PIECES))

        @pl.when(peer != me)
        def _():
            pl.semaphore_signal(barrier, inc=1, device_id={"req": peer}, device_id_type=MESH)

        return carry

    tp_peers = movers.peers()
    for peer in tp_peers:
        pl.semaphore_signal(barrier, inc=1, device_id={"tp": peer}, device_id_type=MESH)
    lax.fori_loop(0 if crossing else PIECES, GROUPS, greet, 0)

    loads[0].wait()
    conv_rows[...] = jnp.zeros_like(conv_rows)
    for j in range(MOVE):
        for tap in range(3):
            for part in range(4):
                conv_rows[j, pl.ds(tap * 4 + part, 1), :] = conv[
                    slot[j], tap, :, part * LANES : (part + 1) * LANES
                ]
        conv_out[j] = conv_rows[j].astype(BF16)
    loads[1].wait()

    def pack(piece, carry):
        start = pl.multiple_of(lax.rem(piece, 8) * TILE, TILE)
        for j in range(MOVE):
            rows_out[j, piece] = states[slot[j], piece // 8, pl.ds(start, TILE), :].astype(BF16)
        return carry

    lax.fori_loop(0, PIECES, pack, 0)

    for load in loads[2:7]:
        load.wait()
    fresh[...] = mixed[...].astype(F32)
    latest = [fresh[:, t, :] for t in range(STEPS)]
    gate_rows[...] = jnp.zeros_like(gate_rows)
    for t in range(STEPS):
        for kind in range(2):
            at = t * 4 + kind * 2
            gate_rows[at : at + 2, 0:rows] = gates[t, kind]
    columns = gate_rows[...].T

    def both(at):
        return jnp.concatenate(
            [
                jnp.broadcast_to(columns[0:rows, at + h : at + h + 1], (rows, HEAD))
                for h in range(2)
            ],
            axis=1,
        )

    rate = jnp.exp(halves(decay_log[0], decay_log[1], (1, 2 * HEAD)))
    bias = halves(time_bias[0], time_bias[1], (1, 2 * HEAD))
    decays, betas, zs = [], [], []
    for t in range(STEPS):
        a = both(t * 4) + bias
        soft = jnp.maximum(a, 0.0) + jnp.log1p(jnp.exp(-jnp.abs(a)))
        decays.append(jnp.exp(-rate * soft))
        betas.append(jax.nn.sigmoid(both(t * 4 + 2)))
        zs.append(zgate[:, t, :].astype(F32))
    spread = gain[...]

    left[...] = jnp.zeros_like(left)
    right[...] = jnp.zeros_like(right)
    window = [conv[:, tap, 0, :] for tap in range(3)] + latest
    queries, keys, values = convolved(window, weight)
    read_side(left, queries, keys)
    for r in range(rows):
        lhs = left[:, r, :].astype(BF16)
        for h in range(2):
            block = states[r, h]
            high = block.astype(BF16)
            low = (block - high.astype(F32)).astype(BF16)
            product = jnp.dot(lhs, high, preferred_element_type=F32) + jnp.dot(
                lhs, low, preferred_element_type=F32
            )
            solved[r, :, h * HEAD : (h + 1) * HEAD] = product[0:8] + product[8:16]
    gram = products(queries, keys)
    writes, carried = solve(solved, flat, gram, values, decays, betas, zs, spread)
    write_side(left, right, keys, writes, carried)

    def picked(value):
        at_row = lax.broadcasted_iota(jnp.int32, value.shape, 0)
        target = (8, value.shape[1])
        at_out = lax.broadcasted_iota(jnp.int32, target, 0)
        result = jnp.zeros(target, F32)
        for j in range(MOVE):
            row = jnp.sum(jnp.where(at_row == slot[j], value, 0.0), axis=0, keepdims=True)
            result = jnp.where(at_out == j, jnp.broadcast_to(row, target), result)
        return result

    latest_m = [picked(value) for value in latest]
    decays_m = [picked(value) for value in decays]
    betas_m = [picked(value) for value in betas]
    zs_m = [picked(value) for value in zs]

    pl.semaphore_wait(barrier, (GROUPS if crossing else PIECES) - 1 + len(tp_peers))

    def first(j, piece, peer):
        return pltpu.make_async_remote_copy(
            src_ref=rows_out.at[j, piece], dst_ref=held[j].at[mine], send_sem=send1.at[j, piece],
            recv_sem=recv1.at[j, mine], device_id={"req": peer}, device_id_type=MESH,
        )

    def conv_first(j, peer):
        return pltpu.make_async_remote_copy(
            src_ref=conv_out.at[j], dst_ref=conv_held.at[mine], send_sem=csend1.at[j],
            recv_sem=crecv1.at[mine], device_id={"req": peer}, device_id_type=MESH,
        )

    for j in range(MOVE):
        peer = member(first_half(j), CONV_PIECE[j])

        @pl.when(peer != me)
        def _():
            conv_first(j, peer).start()

        @pl.when(peer == me)
        def _():
            conv_held[mine] = conv_out[j]

    for j in range(MOVE):

        def send_piece(k, carry):
            piece = lax.rem(mine + k, PIECES)
            peer = member(first_half(j), piece)

            @pl.when(peer != me)
            def _():
                first(j, piece, peer).start()

            @pl.when(peer == me)
            def _():
                held[j][mine] = rows_out[j, piece]

            return carry

        lax.fori_loop(0, PIECES, send_piece, 0)

    loads[7].wait()
    everyone.begin(jnp.concatenate([flat[0], flat[1]], axis=1).astype(BF16))
    for r in range(rows):
        new = list(updated(left, right, r, [states[r, h] for h in range(2)]))
        for h in range(2):
            states[r, h] = new[h]
    stores = [
        pltpu.make_async_copy(src, dst, store_sems.at[at])
        for at, (src, dst) in enumerate(
            (
                (states, states_out.at[pl.ds(0, rows)]), (everyone.blocks, hidden_all),
                (moved, states_out.at[pl.ds(rows, MOVE)]),
                (movers.blocks, hidden_moved),
            )
        )
    ]
    stores[0].start()
    everyone.along_x()

    def second(j, number):
        return pltpu.make_async_remote_copy(
            src_ref=turned.at[j, number], dst_ref=landed.at[j, mine], send_sem=send2.at[j, number],
            recv_sem=recv2.at[j, mine], device_id={"req": member(half, number)}, device_id_type=MESH,
        )

    def conv_second(j, number):
        return pltpu.make_async_remote_copy(
            src_ref=conv_turned.at[number], dst_ref=conv_landed.at[j], send_sem=csend2.at[number],
            recv_sem=crecv2.at[j], device_id={"req": member(half, number)}, device_id_type=MESH,
        )

    for j in streams:

        def wait_first(k, carry):
            number = lax.rem(mine + k, PIECES)
            source = member(first_half(j), number)

            @pl.when(source != me)
            def _():
                pltpu.make_async_remote_copy(
                    src_ref=rows_out.at[j, 0], dst_ref=held[j].at[number], send_sem=send1.at[j, 0],
                    recv_sem=recv1.at[j, number], device_id={"req": source}, device_id_type=MESH,
                ).wait_recv()

            return carry

        lax.fori_loop(0, PIECES, wait_first, 0)

        def turn(k, carry):
            number = lax.rem(mine + k, PIECES)
            source = partner[order[j], member(half, number)]
            turned[j, number] = held[j][number_of(source)]

            @pl.when(k > 0)
            def _():
                second(j, number).start()

            return carry

        lax.fori_loop(0, PIECES, turn, 0)
        landed[j, mine] = turned[j, mine]

        @pl.when(mine == CONV_PIECE[j])
        def _():
            def wait_conv(k, carry):
                number = lax.rem(mine + k, PIECES)
                source = member(first_half(j), number)

                @pl.when(source != me)
                def _():
                    pltpu.make_async_remote_copy(
                        src_ref=conv_out.at[0], dst_ref=conv_held.at[number], send_sem=csend1.at[0],
                        recv_sem=crecv1.at[number], device_id={"req": source}, device_id_type=MESH,
                    ).wait_recv()

                return carry

            lax.fori_loop(0, PIECES, wait_conv, 0)

            def turn_conv(k, carry):
                number = lax.rem(mine + k, PIECES)
                source = partner[order[j], member(half, number)]
                conv_turned[number] = conv_held[number_of(source)]

                @pl.when(k > 0)
                def _():
                    conv_second(j, number).start()

                return carry

            lax.fori_loop(0, PIECES, turn_conv, 0)
            conv_landed[j] = conv_turned[mine]

    everyone.along_z()

    for j in range(MOVE):
        @pl.when(mine != CONV_PIECE[j])
        def _():
            conv_second(j, CONV_PIECE[j]).wait_recv()

    at_out = lax.broadcasted_iota(jnp.int32, (8, LANES), 0)
    window_m = []
    for tap in range(3):
        parts = []
        for part in range(4):
            at = tap * 4 + part
            value = jnp.zeros((8, LANES), F32)
            for j in range(MOVE):
                row = conv_landed[j].astype(F32)[at : at + 1, :]
                value = jnp.where(at_out == j, jnp.broadcast_to(row, (8, LANES)), value)
            parts.append(value)
        window_m.append(jnp.concatenate(parts, axis=1))
    left_m[...] = jnp.zeros_like(left_m)
    right_m[...] = jnp.zeros_like(right_m)
    solved_m[...] = jnp.zeros_like(solved_m)
    queries, keys, values = convolved(window_m + latest_m, weight)
    read_side(left_m, queries, keys)
    gram = products(queries, keys)

    for j in streams:

        def wait_second(k, carry):
            piece = lax.rem(mine + k, PIECES)
            pltpu.make_async_remote_copy(
                src_ref=turned.at[j, 0], dst_ref=landed.at[j, piece], send_sem=send2.at[j, 0],
                recv_sem=recv2.at[j, piece], device_id={"req": member(half, piece)},
                device_id_type=MESH,
            ).wait_recv()
            return carry

        lax.fori_loop(1, PIECES, wait_second, 0)
        lhs = left_m[:, j, :].astype(BF16)
        for h in range(2):
            block = landed[j, h * 8 : (h + 1) * 8].reshape(HEAD, HEAD)
            product = jnp.dot(lhs, block, preferred_element_type=F32)
            solved_m[j, :, h * HEAD : (h + 1) * HEAD] = product[0:8] + product[8:16]

    writes, carried = solve(
        solved_m, flat_m, gram, values, decays_m, betas_m, zs_m, spread
    )
    movers.begin(jnp.concatenate([flat_m[0, 0:16], flat_m[1, 0:16]], axis=1).astype(BF16))
    write_side(left_m, right_m, keys, writes, carried)
    movers.along_z()
    everyone.back_x()
    for j in range(MOVE):
        blocks = [
            landed[j, h * 8 : (h + 1) * 8].reshape(HEAD, HEAD).astype(F32) for h in range(2)
        ]
        for h, new in enumerate(updated(left_m, right_m, j, blocks)):
            moved[j, h] = new
    stores[2].start()
    everyone.back_core()

    for j in range(MOVE):

        def done_first(piece, carry):
            peer = member(first_half(j), piece)

            @pl.when(peer != me)
            def _():
                first(j, piece, peer).wait_send()

            return carry

        lax.fori_loop(0, PIECES, done_first, 0)
        peer = member(first_half(j), CONV_PIECE[j])

        @pl.when(peer != me)
        def _():
            conv_first(j, peer).wait_send()

        def done_second(k, carry):
            second(j, lax.rem(mine + k, PIECES)).wait_send()
            return carry

        lax.fori_loop(1, PIECES, done_second, 0)

        @pl.when(mine == CONV_PIECE[j])
        def _():
            def done_conv(k, carry):
                conv_second(j, lax.rem(mine + k, PIECES)).wait_send()
                return carry

            lax.fori_loop(1, PIECES, done_conv, 0)

    everyone.end()
    stores[1].start()
    everyone.drain()
    movers.back()
    movers.end()
    stores[3].start()
    movers.drain()
    for store in stores:
        store.wait()


def decode(
    crossing, slots, partner, decay_log, time_bias, state, conv, mixed, gates, zgate, weight, gain, out_weight
):
    rows = state.shape[0]
    width = out_weight.shape[1] // 8
    tile = (TILE, LANES)
    dma = pltpu.SemaphoreType.DMA
    smem = pl.BlockSpec(memory_space=pltpu.SMEM)
    anywhere = pl.BlockSpec(memory_space=pl.ANY)
    arrays = (state, conv, mixed, gates, zgate, weight, gain, out_weight)

    def working(count, padded):
        return [
            VMEM((16, padded, HEAD), F32),
            VMEM((16, padded, 2 * HEAD), F32),
            VMEM((count, 8, 2 * HEAD), F32),
            VMEM((2, count * STEPS, HEAD), F32),
        ]

    return pl.pallas_call(
        functools.partial(decode_kernel, crossing),
        out_shape=(
            jax.ShapeDtypeStruct((rows + MOVE,) + state.shape[1:], F32),
            jax.ShapeDtypeStruct((8, rows * STEPS, width), BF16),
            jax.ShapeDtypeStruct((8, TILE, width), BF16),
        ),
        in_specs=[smem] * 4 + [anywhere] * len(arrays),
        out_specs=(anywhere,) * 3,
        scratch_shapes=[VMEM(state.shape, F32), VMEM((MOVE,) + state.shape[1:], F32), dma((4,))]
        + [VMEM(a.shape, a.dtype) for a in arrays[1:]]
        + [dma((len(arrays),)), VMEM(mixed.shape, F32), VMEM((LANES, LANES), F32)]
        + working(rows, 16)
        + working(8, 8)
        + [
            VMEM((MOVE, PIECES) + tile, BF16),
            VMEM((MOVE,) + tile, F32),
            VMEM((MOVE,) + tile, BF16),
            VMEM((PIECES,) + tile, BF16),
            VMEM((PIECES,) + tile, BF16),
            VMEM((PIECES,) + tile, BF16),
            VMEM((PIECES,) + tile, BF16),
            VMEM((MOVE, PIECES) + tile, BF16),
            VMEM((PIECES,) + tile, BF16),
            VMEM((MOVE, PIECES) + tile, BF16),
            VMEM((MOVE,) + tile, BF16),
            dma((MOVE, PIECES)), dma((MOVE, PIECES)), dma((MOVE,)), dma((PIECES,)),
            dma((MOVE, PIECES)), dma((MOVE, PIECES)), dma((PIECES,)), dma((MOVE,)),
        ]
        + Reduction.scratch(rows * STEPS, width)
        + ShortReduction.scratch(TILE, width),
        compiler_params=pltpu.CompilerParams(
            collective_id=crossing, has_side_effects=True, vmem_limit_bytes=58 << 20
        ),
        name="decode",
    )(slots, partner, decay_log, time_bias, *arrays)


def place_kernel(
    slots, partner, states, hidden_all, hidden_moved, mixed, hidden, new_state, new_conv,
    latest, fresh, out, load_sem, store_sems,
):
    rows = mixed.shape[0]
    width = hidden_all.shape[2]
    slot = [slots[0, at] for at in ordered(partner)]
    load = pltpu.make_async_copy(mixed, latest, load_sem)
    load.start()
    stores = []
    for r in range(rows):
        source = r
        for j in range(MOVE):
            source = jnp.where(slot[j] == r, rows + j, source)
        stores.append(pltpu.make_async_copy(states.at[source], new_state.at[r], store_sems.at[r]))
        stores[r].start()
    stores.append(pltpu.make_async_copy(fresh, new_conv, store_sems.at[rows]))
    for block in range(8):
        cut = pl.ds(block * width, width)
        stores.append(
            pltpu.make_async_copy(
                out.at[:, :, cut], hidden.at[:, :, cut], store_sems.at[rows + 1 + block]
            )
        )
    for block in range(8):
        cut = slice(block * width, (block + 1) * width)
        stay = hidden_all[block].astype(F32)
        came = hidden_moved[block].astype(F32)
        for r in range(rows):
            value = stay[r * STEPS : (r + 1) * STEPS, :]
            for j in range(MOVE):
                value = jnp.where(slot[j] == r, came[j * STEPS : (j + 1) * STEPS, :], value)
            out[r, :, cut] = value.astype(BF16)
        stores[rows + 1 + block].start()
    load.wait()
    values = latest[...].astype(F32)
    for tap in range(3):
        fresh[:, tap, 0, :] = values[:, tap + 1, :]
    stores[rows].start()
    for store in stores:
        store.wait()


def place(slots, partner, states, hidden_all, hidden_moved, mixed):
    rows = mixed.shape[0]
    dma = pltpu.SemaphoreType.DMA
    anywhere = pl.BlockSpec(memory_space=pl.ANY)
    vmem = pl.BlockSpec(memory_space=VMEM)
    hidden = (rows, STEPS, 8 * hidden_all.shape[2])
    conv = (rows, TAPS - 1, 1, mixed.shape[2])
    return pl.pallas_call(
        place_kernel,
        out_shape=(
            jax.ShapeDtypeStruct(hidden, BF16),
            jax.ShapeDtypeStruct((rows,) + states.shape[1:], F32),
            jax.ShapeDtypeStruct(conv, F32),
        ),
        in_specs=[pl.BlockSpec(memory_space=pltpu.SMEM)] * 2 + [vmem] * 3 + [anywhere],
        out_specs=(anywhere,) * 3,
        scratch_shapes=[
            VMEM(mixed.shape, BF16), VMEM(conv, F32), VMEM(hidden, BF16), dma, dma((rows + 9,)),
        ],
        compiler_params=pltpu.CompilerParams(vmem_limit_bytes=40 << 20),
        name="place",
    )(slots, partner, states, hidden_all, hidden_moved, mixed)


def per_device(
    state,
    conv_state,
    mixed,
    gates,
    output_gate,
    conv_weight,
    decay_log,
    time_bias,
    norm_gain,
    out_weight,
    partner,
    moved_slots,
):
    fresh = mixed.reshape(mixed.shape[0], mixed.shape[1], mixed.shape[3])
    masks = partner.T
    states, hidden_all, hidden_moved = lax.switch(
        jnp.sum(lax.rem(partner[0] // 4, 2)),
        [functools.partial(decode, crossing) for crossing in range(MOVE + 1)],
        moved_slots, masks, decay_log, time_bias, state, conv_state.transpose(0, 2, 1, 3),
        fresh, gates.transpose(1, 2, 3, 0), output_gate, conv_weight, norm_gain.reshape(1, -1),
        out_weight,
    )
    hidden, new_state, new_conv = place(
        moved_slots, masks, states, hidden_all, hidden_moved, fresh
    )
    return (hidden, new_state, new_conv.transpose(0, 2, 1, 3))


def solution(mesh):
    placed = (
        P("req", "tp", None, None),
        P("req", "tp", None, None),
        P("req", None, "tp", None),
        P("req", None, None, "tp"),
        P("req", None, "tp"),
        P("tp", None, None),
        P("tp"),
        P("tp"),
        P(),
        P("tp", None),
        P(),
        P("req", None),
    )
    return jax.shard_map(
        per_device,
        mesh=mesh,
        in_specs=placed,
        out_specs=(P("req", None, None), P("req", "tp", None, None), P("req", "tp", None, None)),
        check_vma=False,
    )
```
